32 devices in a mesh: groups: 2 (over x), rows: 8 (over z, y), cols: 2 (over core).
Axes of the slice: x: 2, y: 2, z: 4, core: 2. Of those that a mesh axis runs over, the one named last changes fastest.
Arguments:
- features: float32 [8192, 512], P(('groups', 'rows'), 'cols'), parts along dimension 0, may hold values from -6 to 6
- tile_cols: int32 [64, 16], P(('groups', 'rows')), parts along dimension 0, may hold values from 0 to 31, as said below
- tile_edges: float32 [64, 16, 128, 128], P(('groups', 'rows')), parts along dimension 0, may hold values from 0 to 1, as said below
- degrees: int32 [8192], P(('groups', 'rows')), parts along dimension 0, may hold values from 16 to 64
- w_self: float32 [512, 512], P(None, 'cols'), may hold values from -0.25 to 0.25
- w_neigh: float32 [512, 512], P(None, 'cols'), may hold values from -3 to 3
- bias: float32 [512], P('cols'), may hold values from -3 to 3
- cotangent: float32 [8192, 512], P(('groups', 'rows'), 'cols'), parts along dimension 0, may hold values from -6 to 6
Outputs:
- hidden: float32 [8192, 512], P(('groups', 'rows'), 'cols'), parts along dimension 0
- grad_features: float32 [8192, 512], P(('groups', 'rows'), 'cols'), parts along dimension 0
- grad_self: float32 [1024, 512], P('groups', 'cols'), parts along dimension 0
- grad_neigh: float32 [1024, 512], P('groups', 'cols'), parts along dimension 0
- grad_bias: float32 [1024], P(('groups', 'cols')), parts along dimension 0
The draws below stay inside these ranges and needn't reach their ends.
There are 2 independent parts, one for each index of `groups`. The reference program is written for one: setup_inputs(seed, part) draws one part's arguments, and reference() takes and returns one part's arrays. A program takes and returns all parts, laid end to end along the dimension named above; an argument that names none is the same for every part. Nothing has to cross between parts.
Inputs may be any that keep to these rules, and one draw needn't show every extreme that they name: `tile_cols`: row block b lies on device b // 4 of the axis. The first 10 tiles of each row block name blocks of its own device, the others blocks of other devices; the 24 tiles of one device that name other devices name any one other device at most 4 times, and exactly 4 times for some. `tile_edges`: every entry is 0 or 1.
All inputs are finite; a program needn't handle non-finite values.
Results may differ from the reference program's by a relative error of at most 0.00016.
Values sent between devices are 32-bit elements; how exact they have to be, the bound alone decides.
No kernel may reach another device: no remote copies, remote signals or barrier semaphores. Data moves between devices by JAX's collectives and lax.ppermute only.
A program may use at most 128 MiB of HBM per device.

```python
import jax
import jax.numpy as jnp
from jax import lax

F = 512
TILE = 128
BLK_DEV = 4
K = 16
K_LOCAL = 10
REMOTE = 24
CAP = 4
NBLK = 32
NODES = 4096
N_ROWS = 8


def draw_tile_cols(key, part):
    key = jax.random.fold_in(key, 11)
    first, second, third = jax.random.split(key, 3)
    devices = jnp.arange(N_ROWS)
    near = jax.random.randint(first, (N_ROWS, BLK_DEV, K_LOCAL), 0, BLK_DEV) + devices[:, None, None] * BLK_DEV
    keys = jax.random.split(second, N_ROWS)
    slots = jax.vmap(lambda k: jax.random.permutation(k, CAP * (N_ROWS - 1)))(keys)[:, :REMOTE]
    owner = (devices[:, None] + slots // CAP + 1) % N_ROWS
    far = owner * BLK_DEV + jax.random.randint(third, (N_ROWS, REMOTE), 0, BLK_DEV)
    far = far.reshape(N_ROWS, BLK_DEV, K - K_LOCAL)
    return jnp.concatenate([near, far], axis=2).reshape(NBLK, K).astype(jnp.int32)


def draw_tile_edges(key, part):
    key = jax.random.fold_in(key, 23)
    edges = jax.random.bernoulli(key, 1.0 / 64.0, (NBLK, K, TILE, TILE))
    return edges.astype(jnp.float32)


def plant(drawn, own_key, least, high):
    longest = drawn.shape.index(max(drawn.shape))
    spots = []
    for shift in (0, 1):
        where = [jax.random.randint(jax.random.fold_in(own_key, axis), (), 0, length) for axis, length in enumerate(drawn.shape)]
        where[longest] = (where[longest] + shift) % drawn.shape[longest]
        spots.append(tuple(where))
    return drawn.at[spots[0]].set(least).at[spots[1]].set(high)


def steps_of(rng, shape, cuts, smallest, high):
    factor_of = 1.0
    for position, blocks in cuts:
        heights = jax.random.uniform(jax.random.fold_in(jax.random.fold_in(rng, 6), position), (blocks,), jnp.float32, smallest / len(cuts), high / len(cuts))
        factor_of = factor_of * jnp.repeat(jnp.exp(heights), shape[position] // blocks).reshape((-1,) + (1,) * (len(shape) - 1 - position))
    return factor_of


def gaussian(rng, dims, spread, bound, cuts=(), dtype=jnp.bfloat16):
    drawn = spread * jax.random.normal(rng, dims, jnp.float32)
    if cuts:
        drawn = drawn * steps_of(rng, dims, cuts, -0.22, 0.18)
    return jnp.clip(drawn, -bound, bound).astype(dtype)


def setup_inputs(seed: int = 0, part: int = 0) -> dict:
    splits = jax.random.split(jax.random.key(seed), 9)
    part_splits = jax.random.split(jax.random.fold_in(splits[8], part), 9)
    return {
        "features": gaussian(part_splits[0], (NODES, F), 1.0, 6.0, ((0, 8), (1, 2)), jnp.float32),
        "tile_cols": draw_tile_cols(jax.random.fold_in(jax.random.fold_in(splits[8], part), 71), part),
        "tile_edges": draw_tile_edges(jax.random.fold_in(jax.random.fold_in(splits[8], part), 71), part),
        "degrees": plant(jax.random.randint(part_splits[3], (NODES,), max(K * TILE // 128, 1), K * TILE // 32 + 1), jax.random.fold_in(part_splits[3], 1), max(K * TILE // 128, 1), (K * TILE // 32 + 1) - 1).astype(jnp.int32),
        "w_self": gaussian(splits[4], (F, F), F ** -0.5, 0.25, ((1, 2),), jnp.float32),
        "w_neigh": gaussian(splits[5], (F, F), (max(F // 128, 1)) ** -0.5, 3.0, ((1, 2),), jnp.float32),
        "bias": gaussian(splits[6], (F,), 0.5, 3.0, ((0, 2),), jnp.float32),
        "cotangent": gaussian(part_splits[7], (NODES, F), 1.0, 6.0, ((0, 8), (1, 2)), jnp.float32),
    }


def aggregate(features, tile_cols, tile_edges, degrees):
    blocks = features.reshape(NBLK, TILE, F)

    def one_block(items):
        cols, edges = items
        picked = jnp.take(blocks, cols, axis=0)
        return jnp.einsum('kij,kjf->if', edges, picked, precision=lax.Precision.HIGHEST)
    summed = lax.map(one_block, (tile_cols, tile_edges)).reshape(NODES, F)
    return summed / degrees.astype(jnp.float32)[:, None]

def reference(features, tile_cols, tile_edges, degrees, w_self, w_neigh, bias, cotangent):

    def forward(feats, wself, wneigh, offset):
        mean = aggregate(feats, tile_cols, tile_edges, degrees)
        pre = jnp.dot(feats, wself, precision=lax.Precision.HIGHEST)
        pre = pre + jnp.dot(mean, wneigh, precision=lax.Precision.HIGHEST) + offset
        return pre * jax.nn.sigmoid(pre)
    hidden, pullback = jax.vjp(forward, features, w_self, w_neigh, bias)
    grad_features, grad_self, grad_neigh, grad_bias = pullback(cotangent)
    return (hidden, grad_features, grad_self, grad_neigh, grad_bias)
```

```python
import functools

import jax
import jax.numpy as jnp
from jax import lax
from jax.experimental import pallas as pl
from jax.experimental.pallas import tpu as pltpu
from jax.sharding import PartitionSpec as P

F32, BF16 = jnp.float32, jnp.bfloat16
NN = (((1,), (0,)), ((), ()))
NT = (((1,), (1,)), ((), ()))
TN = (((0,), (0,)), ((), ()))


def dot(a, b, dims=NN):
    return lax.dot_general(a, b, dims, preferred_element_type=F32)


def split(v):
    high = v.astype(BF16)
    return high, (v - high.astype(F32)).astype(BF16)


def dot3(a, b, dims=NN):
    ah, al = split(a)
    bh, bl = split(b)
    return dot(ah, bh, dims) + (dot(ah, bl, dims) + dot(al, bh, dims))


def spread(a, x, dims=NN):
    high, low = split(x)
    return dot(a, high, dims) + dot(a, low, dims)


def size(s):
    n = jnp.dtype(s.dtype).itemsize
    for d in s.shape:
        n *= d
    return n


def call(body, out_shape, args, *, flops, prefetch=0, grid=(), in_specs=None, out_specs=None, name, vmem=32):
    outs = out_shape if isinstance(out_shape, (tuple, list)) else (out_shape,)
    moved = sum(size(a) for a in args) + sum(size(o) for o in outs)
    whole = pl.BlockSpec(memory_space=pltpu.VMEM)
    if in_specs is None:
        in_specs = [whole] * (len(args) - prefetch)
    if out_specs is None:
        out_specs = jax.tree.map(lambda _: whole, out_shape)
    return pl.pallas_call(
        body,
        out_shape=out_shape,
        grid_spec=pltpu.PrefetchScalarGridSpec(
            num_scalar_prefetch=prefetch, grid=grid, in_specs=in_specs, out_specs=out_specs
        ),
        compiler_params=pltpu.CompilerParams(vmem_limit_bytes=vmem * 2**20),
        cost_estimate=pl.CostEstimate(flops=int(flops), bytes_accessed=int(moved), transcendentals=0),
        name=name,
    )(*args)


def densify_body(rel, edges, a, at):
    b = pl.program_id(0)
    a[...] = jnp.zeros_like(a)
    at[...] = jnp.zeros_like(at)
    for k in range(edges.shape[1]):
        c = rel[b, k]
        e = edges[0, k]
        a[c] = a[c] + e.astype(BF16)
        at[c] = at[c] + e.T.astype(BF16)


def wide(a, first, blocks):
    return jnp.concatenate([a[first + j] for j in range(blocks)], axis=1)


def gather_step_body(blocks, *refs):
    a, *xs, out = refs
    total = None
    if len(xs) > len(a) // blocks:
        total, xs = xs[-1][...], xs[:-1]
    for i, x in enumerate(xs):
        part = spread(wide(a, i * blocks, blocks), x[...])
        total = part if total is None else total + part
    out[...] = total


def mean_body(blocks, a, xa, xb, total, inverse, out):
    x = jnp.concatenate([xa[...], xb[...]], axis=0)
    s = total[...] + spread(wide(a, 0, blocks), x)
    inv = inverse[...]
    out[...] = s * jnp.concatenate([inv] * (s.shape[1] // inv.shape[1]), axis=1)


def own_product_body(ci, x, w, base, out):
    out[...] = base[...] + dot3(x[...], w[...])


def self_body(ci, x, other, wa, wb, bias, out):
    out[...] = dot3(x[...], wa[...]) + dot3(other[...], wb[...]) + bias[...]


def activate_body(ci, other, w, base, cotangent, hidden, grad_pre):
    pre = base[...] + dot3(other[...], w[...])
    s = jax.nn.sigmoid(pre)
    hidden[...] = pre * s
    grad_pre[...] = cotangent[...] * s * (1.0 + pre * (1.0 - s))


def weight_body(n, place, x, xo, m, mo, g, out):
    gh, gl = split(g[...])
    half = x.shape[1]
    per = 2 * half // n
    tail = jnp.broadcast_to(jnp.sum(g[...], axis=0, keepdims=True), (8, g.shape[1]))
    for src, base in ((x, 0), (xo, half)):
        xh, xl = split(src[...])
        w = dot(xh, gh, TN) + (dot(xh, gl, TN) + dot(xl, gh, TN))
        for i in range(half // per):
            out[place[base // per + i], 0:per] = w[i * per : (i + 1) * per]
    for src, base in ((m, 0), (mo, half)):
        xh, xl = split(src[...])
        w = dot(xh, gh, TN) + (dot(xh, gl, TN) + dot(xl, gh, TN))
        for i in range(half // per):
            out[place[base // per + i], per : 2 * per] = w[i * per : (i + 1) * per]
    for i in range(n):
        out[i, 2 * per :] = tail


def own_back_body(ci, g, ws, wn, direct, mean):
    direct[...] = dot3(g[...], ws[...], NT)
    mean[...] = dot3(g[...], wn[...], NT)


def scaled_body(go, wn, base, inverse, at, high, low, ta, tb):
    inv = inverse[...]
    gm = base[...] + dot3(go[...], wn[...], NT)
    gm = gm * jnp.concatenate([inv] * (gm.shape[1] // inv.shape[1]), axis=1)
    gh, gl = split(gm)
    high[...] = gh
    low[...] = gl
    t = at[...].reshape(-1, at.shape[2])
    t = dot(t, gh) + dot(t, gl)
    h = t.shape[0] // 2
    ta[...] = t[:h]
    tb[...] = t[h:]


def terms_body(at, high, low, out):
    t = at[...].reshape(-1, at.shape[2])
    out[0] = dot(t, high[...]) + dot(t, low[...])


def direct_body(go, ws, base, terms, out):
    out[...] = base[...] + dot3(go[...], ws[...], NT) + terms[0]


def final_body(base, ra, la, rb, lb, out):
    h = ra.shape[0]
    out[0:h] = base[0:h] + (ra[...] + la[...])
    out[h:] = base[h:] + (rb[...] + lb[...])


def assemble_body(where, *refs):
    *shards, out_self, out_neigh = refs
    per = out_self.shape[1]
    for i, s in enumerate(shards):
        out_self[where[i]] = s[0:per]
        out_neigh[where[i]] = s[per : 2 * per]


def local(order, features, tile_cols, tile_edges, degrees, w_self, w_neigh, bias, cotangent):
    blocks, width = tile_cols.shape
    tile = tile_edges.shape[2]
    nodes, half = features.shape
    n = lax.axis_size("rows")
    mid = n // 2
    h = nodes // 2
    sds = jax.ShapeDtypeStruct
    right = [(order[i], order[(i + 1) % n]) for i in range(n)]
    left = [(d, s) for s, d in right]
    send_right = lambda v: lax.ppermute(v, "rows", right)
    send_left = lambda v: lax.ppermute(v, "rows", left)
    swap = lambda v: lax.ppermute(v, "cols", [(0, 1), (1, 0)])
    spots = [0] * n
    for i, r in enumerate(order):
        spots[r] = i
    me = jnp.asarray(spots, jnp.int32)[lax.axis_index("rows")]
    core = lax.axis_index("cols").astype(jnp.int32)
    ci = core.reshape(1)

    def slot_of(spot):
        delta = (spot - me) % n
        return jnp.where(
            delta == 0,
            0,
            jnp.where(delta < mid, 2 * delta, jnp.where(delta == mid, n - 1, 2 * (n - delta) - 1)),
        ).astype(jnp.int32)

    owner = tile_cols // blocks
    spot = jnp.sum(
        jnp.where(owner[..., None] == jnp.arange(n), jnp.asarray(spots, jnp.int32), 0), axis=-1
    )
    rel = slot_of(spot) * blocks + tile_cols % blocks
    inverse = jnp.broadcast_to((1.0 / degrees.astype(F32))[:, None], (nodes, 128))

    a, at = call(
        densify_body,
        (sds((n * blocks, nodes, tile), BF16), sds((n * blocks, tile, nodes), BF16)),
        (rel, tile_edges),
        flops=0,
        prefetch=1,
        grid=(blocks,),
        in_specs=[pl.BlockSpec((1, width, tile, tile), lambda b, _: (b, 0, 0, 0))],
        out_specs=(
            pl.BlockSpec((n * blocks, tile, tile), lambda b, _: (0, b, 0)),
            pl.BlockSpec((n * blocks, tile, tile), lambda b, _: (0, 0, b)),
        ),
        name="densify",
        vmem=32,
    )
    unit = 2 * nodes * nodes * half

    def adjacency(first, count):
        return pl.BlockSpec((count * blocks, nodes, tile), lambda i: (first // count, 0, 0))

    whole = lambda shape: pl.BlockSpec(shape, lambda i, *_: (0,) * len(shape))
    wblock = lambda which: pl.BlockSpec((half, half), lambda i, c: ((c[0] + which) % 2, 0))
    rows_spec = whole((nodes, half))
    out_rows = sds((nodes, half), F32)

    r = l = features
    total = call(
        functools.partial(gather_step_body, blocks),
        out_rows,
        (a, features),
        flops=2 * unit,
        grid=(1,),
        in_specs=[adjacency(0, 1), rows_spec],
        out_specs=rows_spec,
        name="sum_own",
    )
    for s in range(1, mid):
        r, l = send_right(r), send_left(l)
        ins = [pl.BlockSpec((pl.Element(2 * blocks), pl.Element(nodes), pl.Element(tile)),
                            functools.partial(lambda f, i: (f, 0, 0), (2 * s - 1) * blocks))]
        total = call(
            functools.partial(gather_step_body, blocks),
            out_rows,
            (a, r, l, total),
            flops=4 * unit,
            grid=(1,),
            in_specs=ins + [rows_spec] * 3,
            out_specs=rows_spec,
            name="sum_step",
        )
    xa, xb = send_right(r[:h]), send_left(l[h:])

    other_rows = lambda w: lax.dynamic_slice(w, ((1 - core) * half, 0), (half, half))
    x_other = swap(features)
    ws_other, wn_other = swap(other_rows(w_self)), swap(other_rows(w_neigh))
    base = call(
        self_body,
        out_rows,
        (ci, features, x_other, w_self, w_self, bias[None]),
        flops=3 * unit,
        prefetch=1,
        grid=(1,),
        in_specs=[rows_spec, rows_spec, wblock(0), wblock(1), whole((1, half))],
        out_specs=rows_spec,
        name="self_product",
    )

    mean = call(
        functools.partial(mean_body, blocks),
        out_rows,
        (a, xa, xb, total, inverse),
        flops=2 * unit,
        grid=(1,),
        in_specs=[adjacency(n - 1, 1), whole((h, half)), whole((h, half)), rows_spec, whole((nodes, 128))],
        out_specs=rows_spec,
        name="mean",
    )
    mean_other = swap(mean)
    base = call(
        own_product_body,
        out_rows,
        (ci, mean, w_neigh, base),
        flops=1.5 * unit,
        prefetch=1,
        grid=(1,),
        in_specs=[rows_spec, wblock(0), rows_spec],
        out_specs=rows_spec,
        name="mean_product",
    )
    hidden, grad_pre = call(
        activate_body,
        (out_rows, out_rows),
        (ci, mean_other, w_neigh, base, cotangent),
        flops=1.5 * unit,
        prefetch=1,
        grid=(1,),
        in_specs=[rows_spec, wblock(1), rows_spec, rows_spec],
        out_specs=(rows_spec, rows_spec),
        name="activate",
    )
    g_other = swap(grad_pre)
    place = slot_of(jnp.arange(n, dtype=jnp.int32))
    per = 2 * half // n
    shard = 2 * per + 8
    grads = call(
        functools.partial(weight_body, n),
        sds((n, shard, half), F32),
        (place, features, x_other, mean, mean_other, grad_pre),
        flops=6 * unit,
        prefetch=1,
        grid=(1,),
        in_specs=[rows_spec] * 5,
        out_specs=whole((n, shard, half)),
        name="weight_grads",
    )
    direct_own, mean_own = call(
        own_back_body,
        (out_rows, out_rows),
        (ci, grad_pre, w_self, w_neigh),
        flops=3 * unit,
        prefetch=1,
        grid=(1,),
        in_specs=[rows_spec, wblock(0), wblock(0)],
        out_specs=(rows_spec, rows_spec),
        name="back_own",
    )
    part = sds((h, half), F32)
    high, low, ta, tb = call(
        scaled_body,
        (sds((nodes, half), BF16), sds((nodes, half), BF16), part, part),
        (g_other, wn_other, mean_own, inverse, at),
        flops=3.5 * unit,
        grid=(1,),
        in_specs=[
            rows_spec,
            whole((half, half)),
            rows_spec,
            whole((nodes, 128)),
            pl.BlockSpec((blocks, tile, nodes), lambda i: (n - 1, 0, 0)),
        ],
        out_specs=(rows_spec, rows_spec, whole((h, half)), whole((h, half))),
        name="scaled",
    )
    terms = call(
        terms_body,
        sds((n - 1, nodes, half), F32),
        (at, high, low),
        flops=2 * unit * (n - 1),
        grid=(n - 1,),
        in_specs=[pl.BlockSpec((blocks, tile, nodes), lambda i: (n - 2 - i, 0, 0)), rows_spec, rows_spec],
        out_specs=pl.BlockSpec((1, nodes, half), lambda i: (n - 2 - i, 0, 0)),
        name="terms",
    )
    result = call(
        direct_body,
        out_rows,
        (g_other, ws_other, direct_own, terms),
        flops=1.5 * unit,
        grid=(1,),
        in_specs=[rows_spec, whole((half, half)), rows_spec, pl.BlockSpec((1, nodes, half), lambda i: (0, 0, 0))],
        out_specs=rows_spec,
        name="direct",
    )

    cut = per
    wr, wl = send_right(grads[n - 1, :cut]), send_left(grads[n - 1, cut:])
    ra, lb = send_right(ta), send_left(tb)
    rb = la = None
    wra, wrb, wla, wlb = wr, None, None, wl
    add = lambda v, t: t if v is None else v + t
    for d in range(mid - 1, 0, -1):
        to_right, to_left = grads[2 * d], grads[2 * d - 1]
        wr = jnp.concatenate([wra + to_right[:cut], add(wrb, to_right[cut:])], axis=0)
        wl = jnp.concatenate([add(wla, to_left[:cut]), wlb + to_left[cut:]], axis=0)
        wr, wl = send_right(wr), send_left(wl)
        wra, wrb, wla, wlb = wr[:cut], wr[cut:], wl[:cut], wl[cut:]
        ra = send_right(ra + terms[2 * d, :h])
        lb = send_left(lb + terms[2 * d - 1, h:])
        rb = send_right(add(rb, terms[2 * d, h:]))
        la = send_left(add(la, terms[2 * d - 1, :h]))
    mine = grads[0] + wr + wl
    grad_bias = mine[2 * per]
    mine = mine[: 2 * per]
    shards = [mine]
    r = l = mine
    for _ in range(1, mid):
        r, l = send_right(r), send_left(l)
        shards += [r, l]
    shards.append(jnp.concatenate([send_right(r[:per]), send_left(l[per:])], axis=0))
    steps = [0]
    for s in range(1, mid):
        steps += [-s, s]
    steps.append(mid)
    where = ((me + jnp.asarray(steps, jnp.int32)) % n + core * mid) % n
    out_shard = sds((n, per, half), F32)
    grad_self, grad_neigh = call(
        assemble_body,
        (out_shard, out_shard),
        (where.astype(jnp.int32), *shards),
        flops=0,
        prefetch=1,
        grid=(1,),
        in_specs=[whole((2 * per, half))] * n,
        out_specs=(whole((n, per, half)), whole((n, per, half))),
        name="assemble",
    )
    grad_features = call(
        final_body,
        out_rows,
        (result, ra, la, rb, lb),
        flops=0,
        grid=(1,),
        in_specs=[rows_spec] + [whole((h, half))] * 4,
        out_specs=rows_spec,
        name="final",
    )
    return (
        hidden,
        grad_features,
        grad_self.reshape(2 * half, half),
        grad_neigh.reshape(2 * half, half),
        grad_bias,
    )


def solution(mesh):
    n = mesh.shape["rows"]
    coords = [d.coords for d in mesh.devices[0, :, 0]]
    axes = sum(len(set(c)) > 1 for c in zip(*coords))
    if axes > 1:
        order = list(range(0, n, 2)) + list(range(n - 1, 0, -2))
    else:
        order = list(range(n))
    return jax.shard_map(
        functools.partial(local, order),
        mesh=mesh,
        in_specs=(
            P(("groups", "rows"), "cols"),
            P(("groups", "rows"), None),
            P(("groups", "rows"), None, None, None),
            P(("groups", "rows")),
            P(None, "cols"),
            P(None, "cols"),
            P("cols"),
            P(("groups", "rows"), "cols"),
        ),
        out_specs=(
            P(("groups", "rows"), "cols"),
            P(("groups", "rows"), "cols"),
            P("groups", "cols"),
            P("groups", "cols"),
            P(("groups", "cols")),
        ),
        check_vma=False,
    )
```

```python
import functools

import jax
import jax.numpy as jnp
from jax import lax
from jax.experimental import pallas as pl
from jax.experimental.pallas import tpu as pltpu
from jax.sharding import PartitionSpec as P

AG_FULL1 = 1
W_LATE = 0
MERGE1 = 0
WG_FIRST = 0
TERMS_AFTER = 'p'
TAIL = 1
TIE = "all"
COST = 0

F32, BF16 = jnp.float32, jnp.bfloat16
NN = (((1,), (0,)), ((), ()))
NT = (((1,), (1,)), ((), ()))
TN = (((0,), (0,)), ((), ()))


def dot(a, b, dims=NN):
    return lax.dot_general(a, b, dims, preferred_element_type=F32)


def split(v):
    high = v.astype(BF16)
    return high, (v - high.astype(F32)).astype(BF16)


def dot3(a, b, dims=NN):
    ah, al = split(a)
    bh, bl = split(b)
    return dot(ah, bh, dims) + (dot(ah, bl, dims) + dot(al, bh, dims))


def spread(a, x, dims=NN):
    high, low = split(x)
    return dot(a, high, dims) + dot(a, low, dims)


def tie(values):
    return lax.optimization_barrier(values)


def size(s):
    n = jnp.dtype(s.dtype).itemsize
    for d in s.shape:
        n *= d
    return n


def call(body, out_shape, args, *, flops, prefetch=0, grid=(), in_specs=None, out_specs=None, name, vmem=32, aliases=None):
    outs = out_shape if isinstance(out_shape, (tuple, list)) else (out_shape,)
    moved = sum(size(a) for a in args) + sum(size(o) for o in outs)
    whole = pl.BlockSpec(memory_space=pltpu.VMEM)
    if in_specs is None:
        in_specs = [whole] * (len(args) - prefetch)
    if out_specs is None:
        out_specs = jax.tree.map(lambda _: whole, out_shape)
    return pl.pallas_call(
        body,
        out_shape=out_shape,
        grid_spec=pltpu.PrefetchScalarGridSpec(
            num_scalar_prefetch=prefetch, grid=grid, in_specs=in_specs, out_specs=out_specs
        ),
        compiler_params=pltpu.CompilerParams(vmem_limit_bytes=vmem * 2**20),
        cost_estimate=pl.CostEstimate(flops=int(flops * COST) + 1, bytes_accessed=int(moved * COST) + 1, transcendentals=0),
        name=name,
        input_output_aliases=aliases or {},
    )(*args)


def densify_body(rel, edges, a, at):
    b = pl.program_id(0)
    a[...] = jnp.zeros_like(a)
    at[...] = jnp.zeros_like(at)
    for k in range(edges.shape[1]):
        c = rel[b, k]
        e = edges[0, k]
        a[c] = a[c] + e.astype(BF16)
        at[c] = at[c] + e.T.astype(BF16)


def wide(a, first, blocks):
    return jnp.concatenate([a[first + j] for j in range(blocks)], axis=1)


def sum_own_body(blocks, a, x, out):
    out[...] = spread(wide(a, 0, blocks), x[...])


def sum_step_body(blocks, a, ra, rb, la, lb, base, out):
    r = jnp.concatenate([ra[...], rb[...]], axis=0)
    l = jnp.concatenate([la[...], lb[...]], axis=0)
    out[...] = base[...] + (spread(wide(a, 0, blocks), r) + spread(wide(a, blocks, blocks), l))


def mean_body(blocks, a, xa, xb, total, inverse, out):
    x = jnp.concatenate([xa[...], xb[...]], axis=0)
    s = total[...] + spread(wide(a, 0, blocks), x)
    inv = inverse[...]
    out[...] = s * jnp.concatenate([inv] * (s.shape[1] // inv.shape[1]), axis=1)


def own_product_body(ci, x, w, base, out):
    out[...] = base[...] + dot3(x[...], w[...])


def self_body(ci, x, other, wa, wb, bias, out):
    out[...] = dot3(x[...], wa[...]) + dot3(other[...], wb[...]) + bias[...]


def activate_body(ci, other, w, base, cotangent, hidden, grad_pre):
    pre = base[...] + dot3(other[...], w[...])
    s = jax.nn.sigmoid(pre)
    hidden[...] = pre * s
    grad_pre[...] = cotangent[...] * s * (1.0 + pre * (1.0 - s))


def weight_body(n, place, x, xo, m, mo, g, out, first):
    gh, gl = split(g[...])
    half = x.shape[1]
    per = 2 * half // n
    tail = jnp.broadcast_to(jnp.sum(g[...], axis=0, keepdims=True), (8, g.shape[1]))
    for src, base in ((x, 0), (xo, half)):
        xh, xl = split(src[...])
        w = dot(xh, gh, TN) + (dot(xh, gl, TN) + dot(xl, gh, TN))
        for i in range(half // per):
            out[place[base // per + i], 0:per] = w[i * per : (i + 1) * per]
    for src, base in ((m, 0), (mo, half)):
        xh, xl = split(src[...])
        w = dot(xh, gh, TN) + (dot(xh, gl, TN) + dot(xl, gh, TN))
        for i in range(half // per):
            out[place[base // per + i], per : 2 * per] = w[i * per : (i + 1) * per]
    for i in range(n):
        out[i, 2 * per :] = tail
    first[...] = out[n - 1]


def own_back_body(ci, g, ws, wn, direct, mean):
    direct[...] = dot3(g[...], ws[...], NT)
    mean[...] = dot3(g[...], wn[...], NT)


def scaled_body(blocks, go, wn, base, inverse, at, high, low, *out):
    inv = inverse[...]
    gm = base[...] + dot3(go[...], wn[...], NT)
    gm = gm * jnp.concatenate([inv] * (gm.shape[1] // inv.shape[1]), axis=1)
    gh, gl = split(gm)
    high[...] = gh
    low[...] = gl
    cut = blocks // 2

    def part(first, count):
        t = at[first : first + count].reshape(-1, at.shape[2])
        return dot(t, gh) + dot(t, gl)

    if len(out) == 2:
        h = out[0].shape[0] // 2
        out[0][0:h] = part(2 * blocks, cut)
        out[0][h:] = part(blocks + cut, blocks - cut)
        out[1][0:h] = part(0, cut)
        out[1][h:] = part(2 * blocks + cut, blocks - cut)
    else:
        ta, tb, second_right, second_left = out
        ta[...] = part(2 * blocks, cut)
        tb[...] = part(2 * blocks + cut, blocks - cut)
        second_right[...] = part(blocks + cut, blocks - cut)
        second_left[...] = part(0, cut)


def terms_body(at, high, low, out):
    t = at[...].reshape(-1, at.shape[2])
    out[0] = dot(t, high[...]) + dot(t, low[...])


def direct_body(go, ws, base, terms, out):
    out[...] = base[...] + dot3(go[...], ws[...], NT) + terms[0]


def join_body(to_right, to_left, *refs):
    *came, out_right, out_left = refs
    out_right[...] = to_right[0] + came[0][...] if came else to_right[0]
    out_left[...] = to_left[0] + came[1][...] if len(came) > 1 else to_left[0]


def cut_body(r, l, ra, rb, la, lb):
    h = ra.shape[0]
    ra[...] = r[0:h]
    rb[...] = r[h:]
    la[...] = l[0:h]
    lb[...] = l[h:]


def mine_body(own, r, l, out, out_bias):
    total = own[0] + (r[...] + l[...])
    rows = out.shape[0]
    out[...] = total[0:rows]
    out_bias[...] = total[rows : rows + 1]


def final_body(base, ra, la, rb, lb, out):
    h = ra.shape[0]
    out[0:h] = base[0:h] + (ra[...] + la[...])
    out[h:] = base[h:] + (rb[...] + lb[...])


def assemble_body(where, *refs):
    *shards, out_self, out_neigh = refs
    per = out_self.shape[1]
    for i, s in enumerate(shards):
        out_self[where[i]] = s[0:per]
        out_neigh[where[i]] = s[per : 2 * per]


def place_body(where, late, _self, _neigh, out_self, out_neigh):
    per = out_self.shape[1]
    out_self[0] = late[0:per]
    out_neigh[0] = late[per : 2 * per]


def local(order, features, tile_cols, tile_edges, degrees, w_self, w_neigh, bias, cotangent):
    blocks, width = tile_cols.shape
    tile = tile_edges.shape[2]
    nodes, half = features.shape
    n = lax.axis_size("rows")
    mid = n // 2
    h = nodes // 2
    sds = jax.ShapeDtypeStruct
    right = [(order[i], order[(i + 1) % n]) for i in range(n)]
    left = [(d, s) for s, d in right]
    send_right = lambda v: lax.ppermute(v, "rows", right)
    send_left = lambda v: lax.ppermute(v, "rows", left)
    swap = lambda v: lax.ppermute(v, "cols", [(0, 1), (1, 0)])
    spots = [0] * n
    for i, r in enumerate(order):
        spots[r] = i
    me = jnp.asarray(spots, jnp.int32)[lax.axis_index("rows")]
    core = lax.axis_index("cols").astype(jnp.int32)
    ci = core.reshape(1)

    def slot_of(spot):
        delta = (spot - me) % n
        return jnp.where(
            delta == 0,
            0,
            jnp.where(delta < mid, 2 * delta, jnp.where(delta == mid, n - 1, 2 * (n - delta) - 1)),
        ).astype(jnp.int32)

    owner = tile_cols // blocks
    spot = jnp.sum(
        jnp.where(owner[..., None] == jnp.arange(n), jnp.asarray(spots, jnp.int32), 0), axis=-1
    )
    rel = slot_of(spot) * blocks + tile_cols % blocks
    inverse = jnp.broadcast_to((1.0 / degrees.astype(F32))[:, None], (nodes, 128))

    unit = 2 * nodes * nodes * half

    def adjacency(first, count):
        return pl.BlockSpec((count * blocks, nodes, tile), lambda i: (first // count, 0, 0))

    whole = lambda shape: pl.BlockSpec(shape, lambda i, *_: (0,) * len(shape))
    wblock = lambda which: pl.BlockSpec((half, half), lambda i, c: ((c[0] + which) % 2, 0))
    rows_spec = whole((nodes, half))
    out_rows = sds((nodes, half), F32)

    place = slot_of(jnp.arange(n, dtype=jnp.int32))
    half_spec = whole((h, half))

    def sum_step(s, came, total):
        return call(
            functools.partial(sum_step_body, blocks),
            out_rows,
            (a, *came, total),
            flops=4 * unit,
            grid=(1,),
            in_specs=[
                pl.BlockSpec(
                    (pl.Element(2 * blocks), pl.Element(nodes), pl.Element(tile)),
                    lambda i: ((2 * s - 1) * blocks, 0, 0),
                )
            ]
            + [half_spec] * 4
            + [rows_spec],
            out_specs=rows_spec,
            name="sum_step",
        )

    part = sds((h, half), F32)
    if AG_FULL1:
        p = (send_right(features), send_left(features))
    else:
        p = (send_right(features[:h]), send_left(features[h:]))
        q = (send_right(features[h:]), send_left(features[:h]))
    came = [None]
    for s in range(1, mid):
        if s == 1:
            if W_LATE:
                p, ws_, wn_, f_ = tie((p, w_self, w_neigh, features))
            else:
                ws_, wn_, f_ = w_self, w_neigh, features
            other_rows = lambda w: lax.dynamic_slice(w, ((1 - core) * half, 0), (half, half))
            x_other = swap(f_)
            ws_other, wn_other = swap(other_rows(ws_)), swap(other_rows(wn_))
            if W_LATE:
                p, rel, inverse, place = tie((p, rel, inverse, place))
            else:
                p, rel, inverse, place, x_other, ws_other, wn_other = tie(
                    (p, rel, inverse, place, x_other, ws_other, wn_other)
                )
            if AG_FULL1:
                p = call(
                    cut_body,
                    (part,) * 4,
                    p,
                    flops=0,
                    grid=(1,),
                    in_specs=[rows_spec] * 2,
                    out_specs=(half_spec,) * 4,
                    name="cut",
                )
                p, q = (p[0], p[3]), (p[1], p[2])
        elif s == 2:
            rel, came[1] = tie((rel, came[1]))
            a, at = call(
                densify_body,
                (sds((n * blocks, nodes, tile), BF16), sds((n * blocks, tile, nodes), BF16)),
                (rel, tile_edges),
                flops=0,
                prefetch=1,
                grid=(blocks,),
                in_specs=[pl.BlockSpec((1, width, tile, tile), lambda b, _: (b, 0, 0, 0))],
                out_specs=(
                    pl.BlockSpec((n * blocks, tile, tile), lambda b, _: (0, b, 0)),
                    pl.BlockSpec((n * blocks, tile, tile), lambda b, _: (0, 0, b)),
                ),
                name="densify",
                vmem=32,
            )
            p, a, at = tie((p, a, at))
        else:
            total = sum_step(s - 2, came[s - 2], total)
            p, total = tie((p, total))
        first = p
        p = (send_right(p[0]), send_left(p[1]))
        if s == 2:
            features_, first = tie((features, first))
            base = call(
                self_body,
                out_rows,
                (ci, features_, x_other, w_self, w_self, bias[None]),
                flops=3 * unit,
                prefetch=1,
                grid=(1,),
                in_specs=[rows_spec, rows_spec, wblock(0), wblock(1), whole((1, half))],
                out_specs=rows_spec,
                name="self_product",
            )
            total = call(
                functools.partial(sum_own_body, blocks),
                out_rows,
                (a, features_),
                flops=2 * unit,
                grid=(1,),
                in_specs=[adjacency(0, 1), rows_spec],
                out_specs=rows_spec,
                name="sum_own",
            )

            q, base, total, ws_other, wn_other = tie((q, base, total, ws_other, wn_other))
        came.append((first[0], q[0], q[1], first[1]))
        if s < mid - 1:
            q = (send_right(q[0]), send_left(q[1]))
    for s in range(mid - 2, mid):
        total = sum_step(s, came[s], total)
    xa, xb = p

    mean = call(
        functools.partial(mean_body, blocks),
        out_rows,
        (a, xa, xb, total, inverse),
        flops=2 * unit,
        grid=(1,),
        in_specs=[adjacency(n - 1, 1), whole((h, half)), whole((h, half)), rows_spec, whole((nodes, 128))],
        out_specs=rows_spec,
        name="mean",
    )
    mean_other = swap(mean)
    base = call(
        own_product_body,
        out_rows,
        (ci, mean, w_neigh, base),
        flops=1.5 * unit,
        prefetch=1,
        grid=(1,),
        in_specs=[rows_spec, wblock(0), rows_spec],
        out_specs=rows_spec,
        name="mean_product",
    )
    hidden, grad_pre = call(
        activate_body,
        (out_rows, out_rows),
        (ci, mean_other, w_neigh, base, cotangent),
        flops=1.5 * unit,
        prefetch=1,
        grid=(1,),
        in_specs=[rows_spec, wblock(1), rows_spec, rows_spec],
        out_specs=(rows_spec, rows_spec),
        name="activate",
    )
    g_other = swap(grad_pre)
    per = 2 * half // n
    shard = 2 * per + 8
    def weight_grads(grad_pre):
        return call(
            functools.partial(weight_body, n),
            (sds((n, shard, half), F32), sds((shard, half), F32)),
            (place, features, x_other, mean, mean_other, grad_pre),
            flops=6 * unit,
            prefetch=1,
            grid=(1,),
            in_specs=[rows_spec] * 5,
            out_specs=(whole((n, shard, half)), whole((shard, half))),
            name="weight_grads",
        )

    if WG_FIRST:
        grads, first = weight_grads(grad_pre)
        g_other, first = tie((g_other, first))
    direct_own, mean_own = call(
        own_back_body,
        (out_rows, out_rows),
        (ci, grad_pre, w_self, w_neigh),
        flops=3 * unit,
        prefetch=1,
        grid=(1,),
        in_specs=[rows_spec, wblock(0), wblock(0)],
        out_specs=(rows_spec, rows_spec),
        name="back_own",
    )
    part = sds((h, half), F32)
    high, low, *out = call(
        functools.partial(scaled_body, blocks),
        (sds((nodes, half), BF16), sds((nodes, half), BF16)) + ((out_rows,) * 2 if MERGE1 else (part,) * 4),
        (g_other, wn_other, mean_own, inverse, at),
        flops=3.5 * unit,
        grid=(1,),
        in_specs=[
            rows_spec,
            whole((half, half)),
            rows_spec,
            whole((nodes, 128)),
            pl.BlockSpec(
                (pl.Element(3 * blocks), pl.Element(tile), pl.Element(nodes)),
                lambda i: ((n - 3) * blocks, 0, 0),
            ),
        ],
        out_specs=(rows_spec, rows_spec) + ((rows_spec,) * 2 if MERGE1 else (half_spec,) * 4),
        name="scaled",
    )
    ta, tb, *second = out
    if not WG_FIRST:
        grad_pre, ta, tb = tie((grad_pre, ta, tb))
        grads, first = weight_grads(grad_pre)
    p, w = (send_right(ta), send_left(tb)), (send_right(first),)
    if TERMS_AFTER == "w":
        w, high, low = tie((w, high, low))
    elif TERMS_AFTER == "p":
        p, high, low = tie((p, high, low))
    if MERGE1:
        second = p
    terms = call(
        terms_body,
        sds((n - 1, nodes, half), F32),
        (at, high, low),
        flops=2 * unit * (n - 1),
        grid=(n - 1,),
        in_specs=[pl.BlockSpec((blocks, tile, nodes), lambda i: (n - 2 - i, 0, 0)), rows_spec, rows_spec],
        out_specs=pl.BlockSpec((1, nodes, half), lambda i: (n - 2 - i, 0, 0)),
        name="terms",
    )
    result = call(
        direct_body,
        out_rows,
        (g_other, ws_other, direct_own, terms),
        flops=1.5 * unit,
        grid=(1,),
        in_specs=[rows_spec, whole((half, half)), rows_spec, pl.BlockSpec((1, nodes, half), lambda i: (0, 0, 0))],
        out_specs=rows_spec,
        name="direct",
    )

    def join(source, right_at, left_at, rows, came, name, parts=(0, 0)):
        out = sds((rows, half), F32)
        block = lambda at: pl.BlockSpec((1, rows, half), lambda i: (*at, 0))
        part = lambda at: pl.BlockSpec((rows, half), lambda i: (at, 0))
        return call(
            join_body,
            (out, out),
            (source, source, *came),
            flops=0,
            grid=(1,),
            in_specs=[block(right_at), block(left_at)] + [part(at) for _, at in zip(came, parts)],
            out_specs=(whole(out.shape), whole(out.shape)),
            name=name,
        )

    def weight_step(step, w):
        if step < mid:
            d = mid - step
            return join(grads, (2 * d, 0), (2 * d - 1, 0), shard, w, "join_weights")
        if step > mid:
            return w
        mine, bias_sum = call(
            mine_body,
            (sds((2 * per, half), F32), sds((1, half), F32)),
            (grads, *w),
            flops=0,
            grid=(1,),
            in_specs=[pl.BlockSpec((1, shard, half), lambda i: (0, 0, 0))] + [whole((shard, half))] * 2,
            out_specs=(whole((2 * per, half)), whole((1, half))),
            name="mine",
        )
        shards.append(mine)
        biases.append(bias_sum)
        return mine, mine

    shards, biases = [], []
    chains = [p, second]
    for step in range(1, 2 * mid):
        w_in = weight_step(step, w)
        f_in = None
        which = step % 2
        d = mid - (step + 1) // 2
        if step == 1:
            f_in = None if MERGE1 else tuple(second)
        elif step < 2 * mid - 1:
            parts = (0, 0)
            if MERGE1 and d == mid - 1 and not which:
                parts = (0, 1)
            if MERGE1 and d == mid - 2 and which:
                parts = (1, 0)
            at = ((2 * d, which), (2 * d - 1, 1 - which))
            f_in = join(terms, *at, h, chains[which], "join_terms", parts)
        if step == 2:
            result, w_in = tie((result, w_in))
        if f_in is not None and (TIE == "all" or TIE == "even" and not which or TIE == "odd" and which):
            w_in, f_in = tie((w_in, f_in))
        elif f_in is not None and TIE == "f":
            if step > 2:
                f_in, last = tie((f_in, last))
            last = f_in
        w = (send_right(w_in[0]), send_left(w_in[1])) if step < 2 * mid - 1 else (send_right(w_in[0]),)
        if step >= mid:
            shards += w
        if f_in is not None:
            chains[which] = (send_right(f_in[0]), send_left(f_in[1]))
    p, q = chains
    grad_bias = biases[0]

    steps = [0]
    for s in range(1, mid):
        steps += [-s, s]
    steps.append(mid)
    where = ((me + jnp.asarray(steps, jnp.int32)) % n + core * mid) % n
    where = where.astype(jnp.int32)
    grad_features = call(
        final_body,
        out_rows,
        (result, p[0], q[1], q[0], p[1]),
        flops=0,
        grid=(1,),
        in_specs=[rows_spec] + [half_spec] * 4,
        out_specs=rows_spec,
        name="final",
    )
    out_shard = sds((n, per, half), F32)
    *early, late = shards
    grad_self, grad_neigh = call(
        assemble_body,
        (out_shard, out_shard),
        (where, *early),
        flops=0,
        prefetch=1,
        grid=(1,),
        in_specs=[whole((2 * per, half))] * (n - 1),
        out_specs=(whole((n, per, half)), whole((n, per, half))),
        name="assemble",
    )
    if TAIL == 1:
        late, grad_self, grad_neigh, grad_features = tie((late, grad_self, grad_neigh, grad_features))
    elif TAIL == 2:
        late, grad_self, grad_neigh = tie((late, grad_self, grad_neigh))
    last_spec = pl.BlockSpec((1, per, half), lambda i, where: (where[n - 1], 0, 0))
    grad_self, grad_neigh = call(
        place_body,
        (out_shard, out_shard),
        (where, late, grad_self, grad_neigh),
        flops=0,
        prefetch=1,
        grid=(1,),
        in_specs=[whole((2 * per, half))] + [pl.BlockSpec(memory_space=pl.ANY)] * 2,
        out_specs=(last_spec, last_spec),
        name="place_last",
        aliases={2: 0, 3: 1},
    )
    return (
        hidden,
        grad_features,
        grad_self.reshape(2 * half, half),
        grad_neigh.reshape(2 * half, half),
        grad_bias.reshape(half),
    )


def solution(mesh):
    n = mesh.shape["rows"]
    coords = [d.coords for d in mesh.devices[0, :, 0]]
    axes = sum(len(set(c)) > 1 for c in zip(*coords))
    if axes > 1:
        order = list(range(0, n, 2)) + list(range(n - 1, 0, -2))
    else:
        order = list(range(n))
    return jax.shard_map(
        functools.partial(local, order),
        mesh=mesh,
        in_specs=(
            P(("groups", "rows"), "cols"),
            P(("groups", "rows"), None),
            P(("groups", "rows"), None, None, None),
            P(("groups", "rows")),
            P(None, "cols"),
            P(None, "cols"),
            P("cols"),
            P(("groups", "rows"), "cols"),
        ),
        out_specs=(
            P(("groups", "rows"), "cols"),
            P(("groups", "rows"), "cols"),
            P("groups", "cols"),
            P("groups", "cols"),
            P(("groups", "cols")),
        ),
        check_vma=False,
    )
```

```python
import functools

import jax
import jax.numpy as jnp
from jax import lax
from jax.experimental import pallas as pl
from jax.experimental.pallas import tpu as pltpu
from jax.sharding import PartitionSpec as P

AG_FULL1 = 1
W_LATE = 0
MERGE1 = 0
WG_FIRST = 1
TERMS_AFTER = "none"
TAIL = 1
LEAD = 1
TW = 0
TIE = "all"
COST = 0
BASE = 1

F32, BF16 = jnp.float32, jnp.bfloat16
NN = (((1,), (0,)), ((), ()))
NT = (((1,), (1,)), ((), ()))
TN = (((0,), (0,)), ((), ()))


def dot(a, b, dims=NN):
    return lax.dot_general(a, b, dims, preferred_element_type=F32)


def split(v):
    high = v.astype(BF16)
    return high, (v - high.astype(F32)).astype(BF16)


def dot3(a, b, dims=NN):
    ah, al = split(a)
    bh, bl = split(b)
    return dot(ah, bh, dims) + (dot(ah, bl, dims) + dot(al, bh, dims))


def spread(a, x, dims=NN):
    high, low = split(x)
    return dot(a, high, dims) + dot(a, low, dims)


def tie(values):
    return lax.optimization_barrier(values)


def size(s):
    n = jnp.dtype(s.dtype).itemsize
    for d in s.shape:
        n *= d
    return n


def call(body, out_shape, args, *, flops, prefetch=0, grid=(), in_specs=None, out_specs=None, name, vmem=32, aliases=None):
    outs = out_shape if isinstance(out_shape, (tuple, list)) else (out_shape,)
    moved = sum(size(a) for a in args) + sum(size(o) for o in outs)
    whole = pl.BlockSpec(memory_space=pltpu.VMEM)
    if in_specs is None:
        in_specs = [whole] * (len(args) - prefetch)
    if out_specs is None:
        out_specs = jax.tree.map(lambda _: whole, out_shape)
    return pl.pallas_call(
        body,
        out_shape=out_shape,
        grid_spec=pltpu.PrefetchScalarGridSpec(
            num_scalar_prefetch=prefetch, grid=grid, in_specs=in_specs, out_specs=out_specs
        ),
        compiler_params=pltpu.CompilerParams(vmem_limit_bytes=vmem * 2**20),
        cost_estimate=pl.CostEstimate(flops=int(flops * COST) + 1, bytes_accessed=int(moved * COST) + BASE, transcendentals=0),
        name=name,
        input_output_aliases=aliases or {},
    )(*args)


def densify_body(rel, edges, a, at):
    b = pl.program_id(0)
    a[...] = jnp.zeros_like(a)
    at[...] = jnp.zeros_like(at)
    for k in range(edges.shape[1]):
        c = rel[b, k]
        e = edges[0, k]
        a[c] = a[c] + e.astype(BF16)
        at[c] = at[c] + e.T.astype(BF16)


def wide(a, first, blocks):
    return jnp.concatenate([a[first + j] for j in range(blocks)], axis=1)


def sum_own_body(blocks, a, x, out):
    out[...] = spread(wide(a, 0, blocks), x[...])


def sum_step_body(blocks, a, ra, rb, la, lb, base, out):
    r = jnp.concatenate([ra[...], rb[...]], axis=0)
    l = jnp.concatenate([la[...], lb[...]], axis=0)
    out[...] = base[...] + (spread(wide(a, 0, blocks), r) + spread(wide(a, blocks, blocks), l))


def mean_body(blocks, a, xa, xb, total, inverse, out):
    x = jnp.concatenate([xa[...], xb[...]], axis=0)
    s = total[...] + spread(wide(a, 0, blocks), x)
    inv = inverse[...]
    out[...] = s * jnp.concatenate([inv] * (s.shape[1] // inv.shape[1]), axis=1)


def own_product_body(ci, x, w, base, out):
    out[...] = base[...] + dot3(x[...], w[...])


def self_body(ci, x, other, wa, wb, bias, out):
    out[...] = dot3(x[...], wa[...]) + dot3(other[...], wb[...]) + bias[...]


def activate_body(ci, other, w, base, cotangent, hidden, grad_pre):
    pre = base[...] + dot3(other[...], w[...])
    s = jax.nn.sigmoid(pre)
    hidden[...] = pre * s
    grad_pre[...] = cotangent[...] * s * (1.0 + pre * (1.0 - s))


def weight_body(n, place, x, xo, m, mo, g, out, first):
    gh, gl = split(g[...])
    half = x.shape[1]
    per = 2 * half // n
    tail = jnp.broadcast_to(jnp.sum(g[...], axis=0, keepdims=True), (8, g.shape[1]))
    for src, base in ((x, 0), (xo, half)):
        xh, xl = split(src[...])
        w = dot(xh, gh, TN) + (dot(xh, gl, TN) + dot(xl, gh, TN))
        for i in range(half // per):
            out[place[base // per + i], 0:per] = w[i * per : (i + 1) * per]
    for src, base in ((m, 0), (mo, half)):
        xh, xl = split(src[...])
        w = dot(xh, gh, TN) + (dot(xh, gl, TN) + dot(xl, gh, TN))
        for i in range(half // per):
            out[place[base // per + i], per : 2 * per] = w[i * per : (i + 1) * per]
    for i in range(n):
        out[i, 2 * per :] = tail
    first[...] = out[n - 1]


def own_back_body(ci, g, ws, wn, direct, mean):
    direct[...] = dot3(g[...], ws[...], NT)
    mean[...] = dot3(g[...], wn[...], NT)


def scaled_body(blocks, go, wn, base, inverse, at, high, low, *out):
    inv = inverse[...]
    gm = base[...] + dot3(go[...], wn[...], NT)
    gm = gm * jnp.concatenate([inv] * (gm.shape[1] // inv.shape[1]), axis=1)
    gh, gl = split(gm)
    high[...] = gh
    low[...] = gl
    cut = blocks // 2

    def part(first, count):
        t = at[first : first + count].reshape(-1, at.shape[2])
        return dot(t, gh) + dot(t, gl)

    if len(out) == 2:
        h = out[0].shape[0] // 2
        out[0][0:h] = part(2 * blocks, cut)
        out[0][h:] = part(blocks + cut, blocks - cut)
        out[1][0:h] = part(0, cut)
        out[1][h:] = part(2 * blocks + cut, blocks - cut)
    else:
        ta, tb, second_right, second_left = out
        ta[...] = part(2 * blocks, cut)
        tb[...] = part(2 * blocks + cut, blocks - cut)
        second_right[...] = part(blocks + cut, blocks - cut)
        second_left[...] = part(0, cut)


def terms_body(at, high, low, out):
    t = at[...].reshape(-1, at.shape[2])
    out[0] = dot(t, high[...]) + dot(t, low[...])


def direct_body(go, ws, base, terms, out):
    out[...] = base[...] + dot3(go[...], ws[...], NT) + terms[0]


def join_body(to_right, to_left, *refs):
    *came, out_right, out_left = refs
    out_right[...] = to_right[0] + came[0][...] if came else to_right[0]
    out_left[...] = to_left[0] + came[1][...] if len(came) > 1 else to_left[0]


def cut_body(r, l, ra, rb, la, lb):
    h = ra.shape[0]
    ra[...] = r[0:h]
    rb[...] = r[h:]
    la[...] = l[0:h]
    lb[...] = l[h:]


def mine_body(own, r, l, out, out_bias):
    total = own[0] + (r[...] + l[...])
    rows = out.shape[0]
    out[...] = total[0:rows]
    out_bias[...] = total[rows : rows + 1]


def final_body(base, ra, la, rb, lb, out):
    h = ra.shape[0]
    out[0:h] = base[0:h] + (ra[...] + la[...])
    out[h:] = base[h:] + (rb[...] + lb[...])


def assemble_body(where, *refs):
    *shards, out_self, out_neigh = refs
    per = out_self.shape[1]
    for i, s in enumerate(shards):
        out_self[where[i]] = s[0:per]
        out_neigh[where[i]] = s[per : 2 * per]


def place_body(where, late, _self, _neigh, out_self, out_neigh):
    per = out_self.shape[1]
    out_self[0] = late[0:per]
    out_neigh[0] = late[per : 2 * per]


def local(order, features, tile_cols, tile_edges, degrees, w_self, w_neigh, bias, cotangent):
    blocks, width = tile_cols.shape
    tile = tile_edges.shape[2]
    nodes, half = features.shape
    n = lax.axis_size("rows")
    mid = n // 2
    h = nodes // 2
    sds = jax.ShapeDtypeStruct
    right = [(order[i], order[(i + 1) % n]) for i in range(n)]
    left = [(d, s) for s, d in right]
    send_right = lambda v: lax.ppermute(v, "rows", right)
    send_left = lambda v: lax.ppermute(v, "rows", left)
    swap = lambda v: lax.ppermute(v, "cols", [(0, 1), (1, 0)])
    spots = [0] * n
    for i, r in enumerate(order):
        spots[r] = i
    me = jnp.asarray(spots, jnp.int32)[lax.axis_index("rows")]
    core = lax.axis_index("cols").astype(jnp.int32)
    ci = core.reshape(1)

    def slot_of(spot):
        delta = (spot - me) % n
        return jnp.where(
            delta == 0,
            0,
            jnp.where(delta < mid, 2 * delta, jnp.where(delta == mid, n - 1, 2 * (n - delta) - 1)),
        ).astype(jnp.int32)

    owner = tile_cols // blocks
    spot = jnp.sum(
        jnp.where(owner[..., None] == jnp.arange(n), jnp.asarray(spots, jnp.int32), 0), axis=-1
    )
    rel = slot_of(spot) * blocks + tile_cols % blocks
    inverse = jnp.broadcast_to((1.0 / degrees.astype(F32))[:, None], (nodes, 128))

    unit = 2 * nodes * nodes * half

    def adjacency(first, count):
        return pl.BlockSpec((count * blocks, nodes, tile), lambda i: (first // count, 0, 0))

    whole = lambda shape: pl.BlockSpec(shape, lambda i, *_: (0,) * len(shape))
    wblock = lambda which: pl.BlockSpec((half, half), lambda i, c: ((c[0] + which) % 2, 0))
    rows_spec = whole((nodes, half))
    out_rows = sds((nodes, half), F32)

    place = slot_of(jnp.arange(n, dtype=jnp.int32))
    half_spec = whole((h, half))

    def sum_step(s, came, total):
        return call(
            functools.partial(sum_step_body, blocks),
            out_rows,
            (a, *came, total),
            flops=4 * unit,
            grid=(1,),
            in_specs=[
                pl.BlockSpec(
                    (pl.Element(2 * blocks), pl.Element(nodes), pl.Element(tile)),
                    lambda i: ((2 * s - 1) * blocks, 0, 0),
                )
            ]
            + [half_spec] * 4
            + [rows_spec],
            out_specs=rows_spec,
            name="sum_step",
        )

    part = sds((h, half), F32)
    if AG_FULL1:
        p = (send_right(features), send_left(features))
    else:
        p = (send_right(features[:h]), send_left(features[h:]))
        q = (send_right(features[h:]), send_left(features[:h]))
    came = [None]
    for s in range(1, mid):
        if s == 1:
            if W_LATE:
                p, ws_, wn_, f_ = tie((p, w_self, w_neigh, features))
            else:
                ws_, wn_, f_ = w_self, w_neigh, features
            other_rows = lambda w: lax.dynamic_slice(w, ((1 - core) * half, 0), (half, half))
            x_other = swap(f_)
            ws_other, wn_other = swap(other_rows(ws_)), swap(other_rows(wn_))
            if W_LATE:
                p, rel, inverse, place = tie((p, rel, inverse, place))
            else:
                p, rel, inverse, place, x_other, ws_other, wn_other = tie(
                    (p, rel, inverse, place, x_other, ws_other, wn_other)
                )
            if AG_FULL1:
                p = call(
                    cut_body,
                    (part,) * 4,
                    p,
                    flops=0,
                    grid=(1,),
                    in_specs=[rows_spec] * 2,
                    out_specs=(half_spec,) * 4,
                    name="cut",
                )
                p, q = (p[0], p[3]), (p[1], p[2])
        elif s == 2:
            rel, came[1] = tie((rel, came[1]))
            a, at = call(
                densify_body,
                (sds((n * blocks, nodes, tile), BF16), sds((n * blocks, tile, nodes), BF16)),
                (rel, tile_edges),
                flops=0,
                prefetch=1,
                grid=(blocks,),
                in_specs=[pl.BlockSpec((1, width, tile, tile), lambda b, _: (b, 0, 0, 0))],
                out_specs=(
                    pl.BlockSpec((n * blocks, tile, tile), lambda b, _: (0, b, 0)),
                    pl.BlockSpec((n * blocks, tile, tile), lambda b, _: (0, 0, b)),
                ),
                name="densify",
                vmem=32,
            )
            p, a, at = tie((p, a, at))
        else:
            total = sum_step(s - 2, came[s - 2], total)
            p, total = tie((p, total))
        first = p
        p = (send_right(p[0]), send_left(p[1]))
        if s == 2:
            features_, first = tie((features, first))
            base = call(
                self_body,
                out_rows,
                (ci, features_, x_other, w_self, w_self, bias[None]),
                flops=3 * unit,
                prefetch=1,
                grid=(1,),
                in_specs=[rows_spec, rows_spec, wblock(0), wblock(1), whole((1, half))],
                out_specs=rows_spec,
                name="self_product",
            )
            total = call(
                functools.partial(sum_own_body, blocks),
                out_rows,
                (a, features_),
                flops=2 * unit,
                grid=(1,),
                in_specs=[adjacency(0, 1), rows_spec],
                out_specs=rows_spec,
                name="sum_own",
            )

            q, base, total, ws_other, wn_other = tie((q, base, total, ws_other, wn_other))
        came.append((first[0], q[0], q[1], first[1]))
        if s < mid - 1:
            q = (send_right(q[0]), send_left(q[1]))
    for s in range(mid - 2, mid):
        total = sum_step(s, came[s], total)
    xa, xb = p

    mean = call(
        functools.partial(mean_body, blocks),
        out_rows,
        (a, xa, xb, total, inverse),
        flops=2 * unit,
        grid=(1,),
        in_specs=[adjacency(n - 1, 1), whole((h, half)), whole((h, half)), rows_spec, whole((nodes, 128))],
        out_specs=rows_spec,
        name="mean",
    )
    mean_other = swap(mean)
    base = call(
        own_product_body,
        out_rows,
        (ci, mean, w_neigh, base),
        flops=1.5 * unit,
        prefetch=1,
        grid=(1,),
        in_specs=[rows_spec, wblock(0), rows_spec],
        out_specs=rows_spec,
        name="mean_product",
    )
    hidden, grad_pre = call(
        activate_body,
        (out_rows, out_rows),
        (ci, mean_other, w_neigh, base, cotangent),
        flops=1.5 * unit,
        prefetch=1,
        grid=(1,),
        in_specs=[rows_spec, wblock(1), rows_spec, rows_spec],
        out_specs=(rows_spec, rows_spec),
        name="activate",
    )
    g_other = swap(grad_pre)
    per = 2 * half // n
    shard = 2 * per + 8
    def weight_grads(grad_pre):
        return call(
            functools.partial(weight_body, n),
            (sds((n, shard, half), F32), sds((shard, half), F32)),
            (place, features, x_other, mean, mean_other, grad_pre),
            flops=6 * unit,
            prefetch=1,
            grid=(1,),
            in_specs=[rows_spec] * 5,
            out_specs=(whole((n, shard, half)), whole((shard, half))),
            name="weight_grads",
        )

    if WG_FIRST:
        grads, first = weight_grads(grad_pre)
        g_other, first = tie((g_other, first))
    direct_own, mean_own = call(
        own_back_body,
        (out_rows, out_rows),
        (ci, grad_pre, w_self, w_neigh),
        flops=3 * unit,
        prefetch=1,
        grid=(1,),
        in_specs=[rows_spec, wblock(0), wblock(0)],
        out_specs=(rows_spec, rows_spec),
        name="back_own",
    )
    part = sds((h, half), F32)
    high, low, *out = call(
        functools.partial(scaled_body, blocks),
        (sds((nodes, half), BF16), sds((nodes, half), BF16)) + ((out_rows,) * 2 if MERGE1 else (part,) * 4),
        (g_other, wn_other, mean_own, inverse, at),
        flops=3.5 * unit,
        grid=(1,),
        in_specs=[
            rows_spec,
            whole((half, half)),
            rows_spec,
            whole((nodes, 128)),
            pl.BlockSpec(
                (pl.Element(3 * blocks), pl.Element(tile), pl.Element(nodes)),
                lambda i: ((n - 3) * blocks, 0, 0),
            ),
        ],
        out_specs=(rows_spec, rows_spec) + ((rows_spec,) * 2 if MERGE1 else (half_spec,) * 4),
        name="scaled",
    )
    ta, tb, *second = out
    if not WG_FIRST:
        grad_pre, ta, tb = tie((grad_pre, ta, tb))
        grads, first = weight_grads(grad_pre)
    p, w = () if LEAD else (send_right(ta), send_left(tb)), (send_right(first),)
    if TERMS_AFTER == "w":
        w, high, low = tie((w, high, low))
    elif TERMS_AFTER == "p":
        p, high, low = tie((p, high, low))
    if MERGE1:
        second = p
    terms = call(
        terms_body,
        sds((n - 1, nodes, half), F32),
        (at, high, low),
        flops=2 * unit * (n - 1),
        grid=(n - 1,),
        in_specs=[pl.BlockSpec((blocks, tile, nodes), lambda i: (n - 2 - i, 0, 0)), rows_spec, rows_spec],
        out_specs=pl.BlockSpec((1, nodes, half), lambda i: (n - 2 - i, 0, 0)),
        name="terms",
    )
    result = call(
        direct_body,
        out_rows,
        (g_other, ws_other, direct_own, terms),
        flops=1.5 * unit,
        grid=(1,),
        in_specs=[rows_spec, whole((half, half)), rows_spec, pl.BlockSpec((1, nodes, half), lambda i: (0, 0, 0))],
        out_specs=rows_spec,
        name="direct",
    )

    if TW:
        w, terms = tie((w, terms))
    def join(source, right_at, left_at, rows, came, name, parts=(0, 0)):
        out = sds((rows, half), F32)
        block = lambda at: pl.BlockSpec((1, rows, half), lambda i: (*at, 0))
        part = lambda at: pl.BlockSpec((rows, half), lambda i: (at, 0))
        return call(
            join_body,
            (out, out),
            (source, source, *came),
            flops=0,
            grid=(1,),
            in_specs=[block(right_at), block(left_at)] + [part(at) for _, at in zip(came, parts)],
            out_specs=(whole(out.shape), whole(out.shape)),
            name=name,
        )

    def weight_step(step, w):
        if step < mid:
            d = mid - step
            return join(grads, (2 * d, 0), (2 * d - 1, 0), shard, w, "join_weights")
        if step > mid:
            return w
        mine, bias_sum = call(
            mine_body,
            (sds((2 * per, half), F32), sds((1, half), F32)),
            (grads, *w),
            flops=0,
            grid=(1,),
            in_specs=[pl.BlockSpec((1, shard, half), lambda i: (0, 0, 0))] + [whole((shard, half))] * 2,
            out_specs=(whole((2 * per, half)), whole((1, half))),
            name="mine",
        )
        shards.append(mine)
        biases.append(bias_sum)
        return mine, mine

    shards, biases = [], []
    chains = [p, second]
    for step in range(1, 2 * mid):
        w_in = weight_step(step, w)
        f_in = None
        turn = step - LEAD
        which = turn % 2
        d = mid - (turn + 1) // 2
        if turn == 0:
            f_in = ta, tb
        elif turn == 1:
            f_in = None if MERGE1 else tuple(second)
        elif turn < 2 * mid - 1:
            parts = (0, 0)
            if MERGE1 and d == mid - 1 and not which:
                parts = (0, 1)
            if MERGE1 and d == mid - 2 and which:
                parts = (1, 0)
            at = ((2 * d, which), (2 * d - 1, 1 - which))
            f_in = join(terms, *at, h, chains[which], "join_terms", parts)
        if step == 2:
            result, w_in = tie((result, w_in))
        if TIE == "serial" and f_in is not None and step > 1:
            f_in, chains[1 - which], w_seen = tie((f_in, chains[1 - which], w_in))
        elif TIE == "serial2" and f_in is not None and step > 1:
            f_in, chains[1 - which], w_in = tie((f_in, chains[1 - which], w_in))
        elif TIE == "q3" and f_in is not None:
            if step == 3:
                f_in, chains[1 - which] = tie((f_in, chains[1 - which]))
            else:
                f_in, w_in = tie((f_in, w_in))
        elif TIE == "serial3" and f_in is not None and step > 1:
            f_in, chains[1 - which] = tie((f_in, chains[1 - which]))
        elif TIE == "wlead" and f_in is not None:
            f_in, w_prev = tie((f_in, w_prev)) if step > 1 else (f_in, w_in)
        elif f_in is not None and (TIE == "all" or TIE == "even" and not which or TIE == "odd" and which):
            w_in, f_in = tie((w_in, f_in))
        elif f_in is not None and TIE == "f":
            if step > 2:
                f_in, last = tie((f_in, last))
            last = f_in
        w_prev = w_in
        w = (send_right(w_in[0]), send_left(w_in[1])) if step < 2 * mid - 1 else (send_right(w_in[0]),)
        if step >= mid:
            shards += w
        if f_in is not None:
            chains[which] = (send_right(f_in[0]), send_left(f_in[1]))
    p, q = chains
    grad_bias = biases[0]

    steps = [0]
    for s in range(1, mid):
        steps += [-s, s]
    steps.append(mid)
    where = ((me + jnp.asarray(steps, jnp.int32)) % n + core * mid) % n
    where = where.astype(jnp.int32)
    grad_features = call(
        final_body,
        out_rows,
        (result, p[0], q[1], q[0], p[1]),
        flops=0,
        grid=(1,),
        in_specs=[rows_spec] + [half_spec] * 4,
        out_specs=rows_spec,
        name="final",
    )
    out_shard = sds((n, per, half), F32)
    *early, late = shards
    grad_self, grad_neigh = call(
        assemble_body,
        (out_shard, out_shard),
        (where, *early),
        flops=0,
        prefetch=1,
        grid=(1,),
        in_specs=[whole((2 * per, half))] * (n - 1),
        out_specs=(whole((n, per, half)), whole((n, per, half))),
        name="assemble",
    )
    if TAIL == 1:
        late, grad_self, grad_neigh, grad_features = tie((late, grad_self, grad_neigh, grad_features))
    elif TAIL == 2:
        late, grad_self, grad_neigh = tie((late, grad_self, grad_neigh))
    last_spec = pl.BlockSpec((1, per, half), lambda i, where: (where[n - 1], 0, 0))
    grad_self, grad_neigh = call(
        place_body,
        (out_shard, out_shard),
        (where, late, grad_self, grad_neigh),
        flops=0,
        prefetch=1,
        grid=(1,),
        in_specs=[whole((2 * per, half))] + [pl.BlockSpec(memory_space=pl.ANY)] * 2,
        out_specs=(last_spec, last_spec),
        name="place_last",
        aliases={2: 0, 3: 1},
    )
    return (
        hidden,
        grad_features,
        grad_self.reshape(2 * half, half),
        grad_neigh.reshape(2 * half, half),
        grad_bias.reshape(half),
    )


def solution(mesh):
    n = mesh.shape["rows"]
    coords = [d.coords for d in mesh.devices[0, :, 0]]
    axes = sum(len(set(c)) > 1 for c in zip(*coords))
    if axes > 1:
        order = list(range(0, n, 2)) + list(range(n - 1, 0, -2))
    else:
        order = list(range(n))
    return jax.shard_map(
        functools.partial(local, order),
        mesh=mesh,
        in_specs=(
            P(("groups", "rows"), "cols"),
            P(("groups", "rows"), None),
            P(("groups", "rows"), None, None, None),
            P(("groups", "rows")),
            P(None, "cols"),
            P(None, "cols"),
            P("cols"),
            P(("groups", "rows"), "cols"),
        ),
        out_specs=(
            P(("groups", "rows"), "cols"),
            P(("groups", "rows"), "cols"),
            P("groups", "cols"),
            P("groups", "cols"),
            P(("groups", "cols")),
        ),
        check_vma=False,
    )
```

```python
import functools

import jax
import jax.numpy as jnp
from jax import lax
from jax.experimental import pallas as pl
from jax.experimental.pallas import tpu as pltpu
from jax.sharding import PartitionSpec as P

F32, BF16 = jnp.float32, jnp.bfloat16
NN = (((1,), (0,)), ((), ()))
NT = (((1,), (1,)), ((), ()))
TN = (((0,), (0,)), ((), ()))


def dot(a, b, dims=NN):
    return lax.dot_general(a, b, dims, preferred_element_type=F32)


def split(v):
    high = v.astype(BF16)
    return high, (v - high.astype(F32)).astype(BF16)


def dot3(a, b, dims=NN):
    ah, al = split(a)
    bh, bl = split(b)
    return dot(ah, bh, dims) + (dot(ah, bl, dims) + dot(al, bh, dims))


def spread(a, x, dims=NN):
    high, low = split(x)
    return dot(a, high, dims) + dot(a, low, dims)


def tie(values):
    return lax.optimization_barrier(values)


def size(s):
    n = jnp.dtype(s.dtype).itemsize
    for d in s.shape:
        n *= d
    return n


def call(body, out_shape, args, *, flops, prefetch=0, grid=(), in_specs=None, out_specs=None, name, vmem=32, aliases=None):
    outs = out_shape if isinstance(out_shape, (tuple, list)) else (out_shape,)
    moved = sum(size(a) for a in args) + sum(size(o) for o in outs)
    whole = pl.BlockSpec(memory_space=pltpu.VMEM)
    if in_specs is None:
        in_specs = [whole] * (len(args) - prefetch)
    if out_specs is None:
        out_specs = jax.tree.map(lambda _: whole, out_shape)
    return pl.pallas_call(
        body,
        out_shape=out_shape,
        grid_spec=pltpu.PrefetchScalarGridSpec(
            num_scalar_prefetch=prefetch, grid=grid, in_specs=in_specs, out_specs=out_specs
        ),
        compiler_params=pltpu.CompilerParams(vmem_limit_bytes=vmem * 2**20),
        cost_estimate=pl.CostEstimate(flops=1, bytes_accessed=1, transcendentals=0),
        name=name,
        input_output_aliases=aliases or {},
    )(*args)


def densify_body(rel, edges, a, at):
    b = pl.program_id(0)
    a[...] = jnp.zeros_like(a)
    at[...] = jnp.zeros_like(at)
    for k in range(edges.shape[1]):
        c = rel[b, k]
        e = edges[0, k]
        a[c] = a[c] + e.astype(BF16)
        at[c] = at[c] + e.T.astype(BF16)


def wide(a, first, blocks):
    return jnp.concatenate([a[first + j] for j in range(blocks)], axis=1)


def sum_own_body(blocks, a, x, out):
    out[...] = spread(wide(a, 0, blocks), x[...])


def sum_step_body(blocks, a, ra, rb, la, lb, base, out):
    r = jnp.concatenate([ra[...], rb[...]], axis=0)
    l = jnp.concatenate([la[...], lb[...]], axis=0)
    out[...] = base[...] + (spread(wide(a, 0, blocks), r) + spread(wide(a, blocks, blocks), l))


def mean_body(blocks, a, xa, xb, total, inverse, out):
    x = jnp.concatenate([xa[...], xb[...]], axis=0)
    s = total[...] + spread(wide(a, 0, blocks), x)
    inv = inverse[...]
    out[...] = s * jnp.concatenate([inv] * (s.shape[1] // inv.shape[1]), axis=1)


def own_product_body(ci, x, w, base, out):
    out[...] = base[...] + dot3(x[...], w[...])


def self_body(ci, x, other, wa, wb, bias, out):
    out[...] = dot3(x[...], wa[...]) + dot3(other[...], wb[...]) + bias[...]


def activate_body(ci, other, w, base, cotangent, hidden, grad_pre):
    pre = base[...] + dot3(other[...], w[...])
    s = jax.nn.sigmoid(pre)
    hidden[...] = pre * s
    grad_pre[...] = cotangent[...] * s * (1.0 + pre * (1.0 - s))


def weight_body(n, place, x, xo, m, mo, g, out, first):
    gh, gl = split(g[...])
    half = x.shape[1]
    per = 2 * half // n
    tail = jnp.broadcast_to(jnp.sum(g[...], axis=0, keepdims=True), (8, g.shape[1]))
    for src, base in ((x, 0), (xo, half)):
        xh, xl = split(src[...])
        w = dot(xh, gh, TN) + (dot(xh, gl, TN) + dot(xl, gh, TN))
        for i in range(half // per):
            out[place[base // per + i], 0:per] = w[i * per : (i + 1) * per]
    for src, base in ((m, 0), (mo, half)):
        xh, xl = split(src[...])
        w = dot(xh, gh, TN) + (dot(xh, gl, TN) + dot(xl, gh, TN))
        for i in range(half // per):
            out[place[base // per + i], per : 2 * per] = w[i * per : (i + 1) * per]
    for i in range(n):
        out[i, 2 * per :] = tail
    first[...] = out[n - 1]


def own_back_body(ci, g, ws, wn, direct, mean):
    direct[...] = dot3(g[...], ws[...], NT)
    mean[...] = dot3(g[...], wn[...], NT)


def scaled_body(blocks, go, wn, base, inverse, at, high, low, *out):
    inv = inverse[...]
    gm = base[...] + dot3(go[...], wn[...], NT)
    gm = gm * jnp.concatenate([inv] * (gm.shape[1] // inv.shape[1]), axis=1)
    gh, gl = split(gm)
    high[...] = gh
    low[...] = gl
    cut = blocks // 2

    def part(first, count):
        t = at[first : first + count].reshape(-1, at.shape[2])
        return dot(t, gh) + dot(t, gl)

    ta, tb, second_right, second_left = out
    ta[...] = part(2 * blocks, cut)
    tb[...] = part(2 * blocks + cut, blocks - cut)
    second_right[...] = part(blocks + cut, blocks - cut)
    second_left[...] = part(0, cut)


def terms_body(at, high, low, out):
    t = at[...].reshape(-1, at.shape[2])
    out[0] = dot(t, high[...]) + dot(t, low[...])


def direct_body(go, ws, base, terms, out):
    out[...] = base[...] + dot3(go[...], ws[...], NT) + terms[0]


def join_body(to_right, to_left, *refs):
    *came, out_right, out_left = refs
    out_right[...] = to_right[0] + came[0][...] if came else to_right[0]
    out_left[...] = to_left[0] + came[1][...] if len(came) > 1 else to_left[0]


def cut_body(r, l, ra, rb, la, lb):
    h = ra.shape[0]
    ra[...] = r[0:h]
    rb[...] = r[h:]
    la[...] = l[0:h]
    lb[...] = l[h:]


def mine_body(own, r, l, out, out_bias):
    total = own[0] + (r[...] + l[...])
    rows = out.shape[0]
    out[...] = total[0:rows]
    out_bias[...] = total[rows : rows + 1]


def final_body(base, ra, la, rb, lb, out):
    h = ra.shape[0]
    out[0:h] = base[0:h] + (ra[...] + la[...])
    out[h:] = base[h:] + (rb[...] + lb[...])


def assemble_body(where, *refs):
    *shards, out_self, out_neigh = refs
    per = out_self.shape[1]
    for i, s in enumerate(shards):
        out_self[where[i]] = s[0:per]
        out_neigh[where[i]] = s[per : 2 * per]


def place_body(where, late, _self, _neigh, out_self, out_neigh):
    per = out_self.shape[1]
    out_self[0] = late[0:per]
    out_neigh[0] = late[per : 2 * per]


def local(order, features, tile_cols, tile_edges, degrees, w_self, w_neigh, bias, cotangent):
    blocks, width = tile_cols.shape
    tile = tile_edges.shape[2]
    nodes, half = features.shape
    n = lax.axis_size("rows")
    mid = n // 2
    h = nodes // 2
    sds = jax.ShapeDtypeStruct
    right = [(order[i], order[(i + 1) % n]) for i in range(n)]
    left = [(d, s) for s, d in right]
    send_right = lambda v: lax.ppermute(v, "rows", right)
    send_left = lambda v: lax.ppermute(v, "rows", left)
    swap = lambda v: lax.ppermute(v, "cols", [(0, 1), (1, 0)])
    spots = [0] * n
    for i, r in enumerate(order):
        spots[r] = i
    me = jnp.asarray(spots, jnp.int32)[lax.axis_index("rows")]
    core = lax.axis_index("cols").astype(jnp.int32)
    ci = core.reshape(1)

    def slot_of(spot):
        delta = (spot - me) % n
        return jnp.where(
            delta == 0,
            0,
            jnp.where(delta < mid, 2 * delta, jnp.where(delta == mid, n - 1, 2 * (n - delta) - 1)),
        ).astype(jnp.int32)

    owner = tile_cols // blocks
    spot = jnp.sum(
        jnp.where(owner[..., None] == jnp.arange(n), jnp.asarray(spots, jnp.int32), 0), axis=-1
    )
    rel = slot_of(spot) * blocks + tile_cols % blocks
    inverse = jnp.broadcast_to((1.0 / degrees.astype(F32))[:, None], (nodes, 128))

    unit = 2 * nodes * nodes * half

    def adjacency(first, count):
        return pl.BlockSpec((count * blocks, nodes, tile), lambda i: (first // count, 0, 0))

    whole = lambda shape: pl.BlockSpec(shape, lambda i, *_: (0,) * len(shape))
    wblock = lambda which: pl.BlockSpec((half, half), lambda i, c: ((c[0] + which) % 2, 0))
    rows_spec = whole((nodes, half))
    out_rows = sds((nodes, half), F32)

    place = slot_of(jnp.arange(n, dtype=jnp.int32))
    half_spec = whole((h, half))

    def sum_step(s, came, total):
        return call(
            functools.partial(sum_step_body, blocks),
            out_rows,
            (a, *came, total),
            flops=4 * unit,
            grid=(1,),
            in_specs=[
                pl.BlockSpec(
                    (pl.Element(2 * blocks), pl.Element(nodes), pl.Element(tile)),
                    lambda i: ((2 * s - 1) * blocks, 0, 0),
                )
            ]
            + [half_spec] * 4
            + [rows_spec],
            out_specs=rows_spec,
            name="sum_step",
        )

    part = sds((h, half), F32)
    p = (send_right(features), send_left(features))
    came = [None]
    for s in range(1, mid):
        if s == 1:
            other_rows = lambda w: lax.dynamic_slice(w, ((1 - core) * half, 0), (half, half))
            x_other = swap(features)
            ws_other, wn_other = swap(other_rows(w_self)), swap(other_rows(w_neigh))
            p, rel, inverse, place, x_other, ws_other, wn_other = tie(
                (p, rel, inverse, place, x_other, ws_other, wn_other)
            )
            p = call(
                cut_body,
                (part,) * 4,
                p,
                flops=0,
                grid=(1,),
                in_specs=[rows_spec] * 2,
                out_specs=(half_spec,) * 4,
                name="cut",
            )
            p, q = (p[0], p[3]), (p[1], p[2])
        elif s == 2:
            rel, came[1] = tie((rel, came[1]))
            a, at = call(
                densify_body,
                (sds((n * blocks, nodes, tile), BF16), sds((n * blocks, tile, nodes), BF16)),
                (rel, tile_edges),
                flops=0,
                prefetch=1,
                grid=(blocks,),
                in_specs=[pl.BlockSpec((1, width, tile, tile), lambda b, _: (b, 0, 0, 0))],
                out_specs=(
                    pl.BlockSpec((n * blocks, tile, tile), lambda b, _: (0, b, 0)),
                    pl.BlockSpec((n * blocks, tile, tile), lambda b, _: (0, 0, b)),
                ),
                name="densify",
                vmem=32,
            )
            p, a, at = tie((p, a, at))
        else:
            total = sum_step(s - 2, came[s - 2], total)
            p, total = tie((p, total))
        first = p
        p = (send_right(p[0]), send_left(p[1]))
        if s == 2:
            features_, first = tie((features, first))
            base = call(
                self_body,
                out_rows,
                (ci, features_, x_other, w_self, w_self, bias[None]),
                flops=3 * unit,
                prefetch=1,
                grid=(1,),
                in_specs=[rows_spec, rows_spec, wblock(0), wblock(1), whole((1, half))],
                out_specs=rows_spec,
                name="self_product",
            )
            total = call(
                functools.partial(sum_own_body, blocks),
                out_rows,
                (a, features_),
                flops=2 * unit,
                grid=(1,),
                in_specs=[adjacency(0, 1), rows_spec],
                out_specs=rows_spec,
                name="sum_own",
            )

            q, base, total, ws_other, wn_other = tie((q, base, total, ws_other, wn_other))
        came.append((first[0], q[0], q[1], first[1]))
        if s < mid - 1:
            q = (send_right(q[0]), send_left(q[1]))
    for s in range(mid - 2, mid):
        total = sum_step(s, came[s], total)
    xa, xb = p

    mean = call(
        functools.partial(mean_body, blocks),
        out_rows,
        (a, xa, xb, total, inverse),
        flops=2 * unit,
        grid=(1,),
        in_specs=[adjacency(n - 1, 1), whole((h, half)), whole((h, half)), rows_spec, whole((nodes, 128))],
        out_specs=rows_spec,
        name="mean",
    )
    mean_other = swap(mean)
    base = call(
        own_product_body,
        out_rows,
        (ci, mean, w_neigh, base),
        flops=1.5 * unit,
        prefetch=1,
        grid=(1,),
        in_specs=[rows_spec, wblock(0), rows_spec],
        out_specs=rows_spec,
        name="mean_product",
    )
    hidden, grad_pre = call(
        activate_body,
        (out_rows, out_rows),
        (ci, mean_other, w_neigh, base, cotangent),
        flops=1.5 * unit,
        prefetch=1,
        grid=(1,),
        in_specs=[rows_spec, wblock(1), rows_spec, rows_spec],
        out_specs=(rows_spec, rows_spec),
        name="activate",
    )
    g_other = swap(grad_pre)
    per = 2 * half // n
    shard = 2 * per + 8
    grads, first = call(
        functools.partial(weight_body, n),
        (sds((n, shard, half), F32), sds((shard, half), F32)),
        (place, features, x_other, mean, mean_other, grad_pre),
        flops=6 * unit,
        prefetch=1,
        grid=(1,),
        in_specs=[rows_spec] * 5,
        out_specs=(whole((n, shard, half)), whole((shard, half))),
        name="weight_grads",
    )
    g_other, first = tie((g_other, first))
    direct_own, mean_own = call(
        own_back_body,
        (out_rows, out_rows),
        (ci, grad_pre, w_self, w_neigh),
        flops=3 * unit,
        prefetch=1,
        grid=(1,),
        in_specs=[rows_spec, wblock(0), wblock(0)],
        out_specs=(rows_spec, rows_spec),
        name="back_own",
    )
    part = sds((h, half), F32)
    high, low, *out = call(
        functools.partial(scaled_body, blocks),
        (sds((nodes, half), BF16), sds((nodes, half), BF16)) + (part,) * 4,
        (g_other, wn_other, mean_own, inverse, at),
        flops=3.5 * unit,
        grid=(1,),
        in_specs=[
            rows_spec,
            whole((half, half)),
            rows_spec,
            whole((nodes, 128)),
            pl.BlockSpec(
                (pl.Element(3 * blocks), pl.Element(tile), pl.Element(nodes)),
                lambda i: ((n - 3) * blocks, 0, 0),
            ),
        ],
        out_specs=(rows_spec, rows_spec) + (half_spec,) * 4,
        name="scaled",
    )
    ta, tb, *second = out
    w = (send_right(first),)
    terms = call(
        terms_body,
        sds((n - 1, nodes, half), F32),
        (at, high, low),
        flops=2 * unit * (n - 1),
        grid=(n - 1,),
        in_specs=[pl.BlockSpec((blocks, tile, nodes), lambda i: (n - 2 - i, 0, 0)), rows_spec, rows_spec],
        out_specs=pl.BlockSpec((1, nodes, half), lambda i: (n - 2 - i, 0, 0)),
        name="terms",
    )
    result = call(
        direct_body,
        out_rows,
        (g_other, ws_other, direct_own, terms),
        flops=1.5 * unit,
        grid=(1,),
        in_specs=[rows_spec, whole((half, half)), rows_spec, pl.BlockSpec((1, nodes, half), lambda i: (0, 0, 0))],
        out_specs=rows_spec,
        name="direct",
    )

    def join(source, right_at, left_at, rows, came, name):
        out = sds((rows, half), F32)
        block = lambda at: pl.BlockSpec((1, rows, half), lambda i: (*at, 0))
        return call(
            join_body,
            (out, out),
            (source, source, *came),
            flops=0,
            grid=(1,),
            in_specs=[block(right_at), block(left_at)] + [whole((rows, half))] * len(came),
            out_specs=(whole(out.shape), whole(out.shape)),
            name=name,
        )

    def weight_step(step, w):
        if step < mid:
            d = mid - step
            return join(grads, (2 * d, 0), (2 * d - 1, 0), shard, w, "join_weights")
        if step > mid:
            return w
        mine, bias_sum = call(
            mine_body,
            (sds((2 * per, half), F32), sds((1, half), F32)),
            (grads, *w),
            flops=0,
            grid=(1,),
            in_specs=[pl.BlockSpec((1, shard, half), lambda i: (0, 0, 0))] + [whole((shard, half))] * 2,
            out_specs=(whole((2 * per, half)), whole((1, half))),
            name="mine",
        )
        shards.append(mine)
        biases.append(bias_sum)
        return mine, mine

    shards, biases = [], []
    chains = [(), second]
    for step in range(1, 2 * mid):
        w_in = weight_step(step, w)
        f_in = None
        turn = step - 1
        which = turn % 2
        d = mid - (turn + 1) // 2
        if turn == 0:
            f_in = ta, tb
        elif turn == 1:
            f_in = tuple(second)
        elif turn < 2 * mid - 1:
            at = ((2 * d, which), (2 * d - 1, 1 - which))
            f_in = join(terms, *at, h, chains[which], "join_terms")
        if step == 2:
            result, w_in = tie((result, w_in))
        if f_in is not None and step > 1:
            w_in, f_in = tie((w_in, f_in))
        w = (send_right(w_in[0]), send_left(w_in[1])) if step < 2 * mid - 1 else (send_right(w_in[0]),)
        if step >= mid:
            shards += w
        if f_in is not None:
            chains[which] = (send_right(f_in[0]), send_left(f_in[1]))
    p, q = chains
    grad_bias = biases[0]

    steps = [0]
    for s in range(1, mid):
        steps += [-s, s]
    steps.append(mid)
    where = ((me + jnp.asarray(steps, jnp.int32)) % n + core * mid) % n
    where = where.astype(jnp.int32)
    grad_features = call(
        final_body,
        out_rows,
        (result, p[0], q[1], q[0], p[1]),
        flops=0,
        grid=(1,),
        in_specs=[rows_spec] + [half_spec] * 4,
        out_specs=rows_spec,
        name="final",
    )
    out_shard = sds((n, per, half), F32)
    *early, late = shards
    grad_self, grad_neigh = call(
        assemble_body,
        (out_shard, out_shard),
        (where, *early),
        flops=0,
        prefetch=1,
        grid=(1,),
        in_specs=[whole((2 * per, half))] * (n - 1),
        out_specs=(whole((n, per, half)), whole((n, per, half))),
        name="assemble",
    )
    late, grad_self, grad_neigh, grad_features = tie((late, grad_self, grad_neigh, grad_features))
    last_spec = pl.BlockSpec((1, per, half), lambda i, where: (where[n - 1], 0, 0))
    grad_self, grad_neigh = call(
        place_body,
        (out_shard, out_shard),
        (where, late, grad_self, grad_neigh),
        flops=0,
        prefetch=1,
        grid=(1,),
        in_specs=[whole((2 * per, half))] + [pl.BlockSpec(memory_space=pl.ANY)] * 2,
        out_specs=(last_spec, last_spec),
        name="place_last",
        aliases={2: 0, 3: 1},
    )
    return (
        hidden,
        grad_features,
        grad_self.reshape(2 * half, half),
        grad_neigh.reshape(2 * half, half),
        grad_bias.reshape(half),
    )


def solution(mesh):
    n = mesh.shape["rows"]
    coords = [d.coords for d in mesh.devices[0, :, 0]]
    axes = sum(len(set(c)) > 1 for c in zip(*coords))
    if axes > 1:
        order = list(range(0, n, 2)) + list(range(n - 1, 0, -2))
    else:
        order = list(range(n))
    return jax.shard_map(
        functools.partial(local, order),
        mesh=mesh,
        in_specs=(
            P(("groups", "rows"), "cols"),
            P(("groups", "rows"), None),
            P(("groups", "rows"), None, None, None),
            P(("groups", "rows")),
            P(None, "cols"),
            P(None, "cols"),
            P("cols"),
            P(("groups", "rows"), "cols"),
        ),
        out_specs=(
            P(("groups", "rows"), "cols"),
            P(("groups", "rows"), "cols"),
            P("groups", "cols"),
            P("groups", "cols"),
            P(("groups", "cols")),
        ),
        check_vma=False,
    )
```

```python
import functools

import jax
import jax.numpy as jnp
from jax import lax
from jax.experimental import pallas as pl
from jax.experimental.pallas import tpu as pltpu
from jax.sharding import PartitionSpec as P

F32, BF16 = jnp.float32, jnp.bfloat16
NN = (((1,), (0,)), ((), ()))
NT = (((1,), (1,)), ((), ()))
TN = (((0,), (0,)), ((), ()))


def dot(a, b, dims=NN):
    return lax.dot_general(a, b, dims, preferred_element_type=F32)


def split(v):
    high = v.astype(BF16)
    return high, (v - high.astype(F32)).astype(BF16)


def dot3(a, b, dims=NN):
    ah, al = split(a)
    bh, bl = split(b)
    return dot(ah, bh, dims) + (dot(ah, bl, dims) + dot(al, bh, dims))


def spread(a, x, dims=NN):
    high, low = split(x)
    return dot(a, high, dims) + dot(a, low, dims)


def tie(values):
    return lax.optimization_barrier(values)


def size(s):
    n = jnp.dtype(s.dtype).itemsize
    for d in s.shape:
        n *= d
    return n


def call(body, out_shape, args, *, flops, prefetch=0, grid=(), in_specs=None, out_specs=None, name, vmem=12, aliases=None):
    outs = out_shape if isinstance(out_shape, (tuple, list)) else (out_shape,)
    moved = sum(size(a) for a in args) + sum(size(o) for o in outs)
    whole = pl.BlockSpec(memory_space=pltpu.VMEM)
    if in_specs is None:
        in_specs = [whole] * (len(args) - prefetch)
    if out_specs is None:
        out_specs = jax.tree.map(lambda _: whole, out_shape)
    return pl.pallas_call(
        body,
        out_shape=out_shape,
        grid_spec=pltpu.PrefetchScalarGridSpec(
            num_scalar_prefetch=prefetch, grid=grid, in_specs=in_specs, out_specs=out_specs
        ),
        compiler_params=pltpu.CompilerParams(vmem_limit_bytes=vmem * 2**20),
        cost_estimate=pl.CostEstimate(flops=1, bytes_accessed=1, transcendentals=0),
        name=name,
        input_output_aliases=aliases or {},
    )(*args)


def densify_body(rel, edges, a, at):
    b = pl.program_id(0)
    a[...] = jnp.zeros_like(a)
    at[...] = jnp.zeros_like(at)
    for k in range(edges.shape[1]):
        c = rel[b, k]
        e = edges[0, k]
        a[c] = a[c] + e.astype(BF16)
        at[c] = at[c] + e.T.astype(BF16)


def wide(a, first, blocks):
    return jnp.concatenate([a[first + j] for j in range(blocks)], axis=1)


def sum_own_body(blocks, a, x, out):
    out[...] = spread(wide(a, 0, blocks), x[...])


def sum_step_body(blocks, a, ra, rb, la, lb, base, out):
    r = jnp.concatenate([ra[...], rb[...]], axis=0)
    l = jnp.concatenate([la[...], lb[...]], axis=0)
    out[...] = base[...] + (spread(wide(a, 0, blocks), r) + spread(wide(a, blocks, blocks), l))


def mean_body(blocks, a, xa, xb, total, inverse, out):
    x = jnp.concatenate([xa[...], xb[...]], axis=0)
    s = total[...] + spread(wide(a, 0, blocks), x)
    inv = inverse[...]
    out[...] = s * jnp.concatenate([inv] * (s.shape[1] // inv.shape[1]), axis=1)


def own_product_body(ci, x, w, base, out):
    out[...] = base[...] + dot3(x[...], w[...])


def self_body(ci, x, other, wa, wb, bias, out):
    out[...] = dot3(x[...], wa[...]) + dot3(other[...], wb[...]) + bias[...]


def activate_body(ci, other, w, base, cotangent, hidden, grad_pre):
    pre = base[...] + dot3(other[...], w[...])
    s = jax.nn.sigmoid(pre)
    hidden[...] = pre * s
    grad_pre[...] = cotangent[...] * s * (1.0 + pre * (1.0 - s))


def weight_body(n, place, x, xo, m, mo, g, out, first):
    gh, gl = split(g[...])
    half = x.shape[1]
    per = 2 * half // n
    tail = jnp.broadcast_to(jnp.sum(g[...], axis=0, keepdims=True), (8, g.shape[1]))
    for src, base in ((x, 0), (xo, half)):
        xh, xl = split(src[...])
        w = dot(xh, gh, TN) + (dot(xh, gl, TN) + dot(xl, gh, TN))
        for i in range(half // per):
            out[place[base // per + i], 0:per] = w[i * per : (i + 1) * per]
    for src, base in ((m, 0), (mo, half)):
        xh, xl = split(src[...])
        w = dot(xh, gh, TN) + (dot(xh, gl, TN) + dot(xl, gh, TN))
        for i in range(half // per):
            out[place[base // per + i], per : 2 * per] = w[i * per : (i + 1) * per]
    for i in range(n):
        out[i, 2 * per :] = tail
    first[...] = out[n - 1]


def own_back_body(ci, g, ws, wn, direct, mean):
    direct[...] = dot3(g[...], ws[...], NT)
    mean[...] = dot3(g[...], wn[...], NT)


def scaled_body(blocks, go, wn, base, inverse, at, high, low, *out):
    inv = inverse[...]
    gm = base[...] + dot3(go[...], wn[...], NT)
    gm = gm * jnp.concatenate([inv] * (gm.shape[1] // inv.shape[1]), axis=1)
    gh, gl = split(gm)
    high[...] = gh
    low[...] = gl
    cut = blocks // 2

    def part(first, count):
        t = at[first : first + count].reshape(-1, at.shape[2])
        return dot(t, gh) + dot(t, gl)

    ta, tb, second_right, second_left = out
    ta[...] = part(2 * blocks, cut)
    tb[...] = part(2 * blocks + cut, blocks - cut)
    second_right[...] = part(blocks + cut, blocks - cut)
    second_left[...] = part(0, cut)


def terms_body(at, high, low, out):
    t = at[...].reshape(-1, at.shape[2])
    out[0] = dot(t, high[...]) + dot(t, low[...])


def direct_body(go, ws, base, terms, out):
    out[...] = base[...] + dot3(go[...], ws[...], NT) + terms[0]


def join_body(to_right, to_left, *refs):
    *came, out_right, out_left = refs
    out_right[...] = to_right[0] + came[0][...] if came else to_right[0]
    out_left[...] = to_left[0] + came[1][...] if len(came) > 1 else to_left[0]


def cut_body(r, l, ra, rb, la, lb):
    h = ra.shape[0]
    ra[...] = r[0:h]
    rb[...] = r[h:]
    la[...] = l[0:h]
    lb[...] = l[h:]


def mine_body(own, r, l, out, out_bias):
    total = own[0] + (r[...] + l[...])
    rows = out.shape[0]
    out[...] = total[0:rows]
    out_bias[...] = total[rows : rows + 1]


def final_body(base, ra, la, rb, lb, out):
    h = ra.shape[0]
    out[0:h] = base[0:h] + (ra[...] + la[...])
    out[h:] = base[h:] + (rb[...] + lb[...])


def assemble_body(where, *refs):
    *shards, out_self, out_neigh = refs
    per = out_self.shape[1]
    for i, s in enumerate(shards):
        out_self[where[i]] = s[0:per]
        out_neigh[where[i]] = s[per : 2 * per]


def place_body(where, late, _self, _neigh, out_self, out_neigh):
    per = out_self.shape[1]
    out_self[0] = late[0:per]
    out_neigh[0] = late[per : 2 * per]


def local(order, features, tile_cols, tile_edges, degrees, w_self, w_neigh, bias, cotangent):
    blocks, width = tile_cols.shape
    tile = tile_edges.shape[2]
    nodes, half = features.shape
    n = lax.axis_size("rows")
    mid = n // 2
    h = nodes // 2
    sds = jax.ShapeDtypeStruct
    right = [(order[i], order[(i + 1) % n]) for i in range(n)]
    left = [(d, s) for s, d in right]
    send_right = lambda v: lax.ppermute(v, "rows", right)
    send_left = lambda v: lax.ppermute(v, "rows", left)
    swap = lambda v: lax.ppermute(v, "cols", [(0, 1), (1, 0)])
    spots = [0] * n
    for i, r in enumerate(order):
        spots[r] = i
    me = jnp.asarray(spots, jnp.int32)[lax.axis_index("rows")]
    core = lax.axis_index("cols").astype(jnp.int32)
    ci = core.reshape(1)

    def slot_of(spot):
        delta = (spot - me) % n
        return jnp.where(
            delta == 0,
            0,
            jnp.where(delta < mid, 2 * delta, jnp.where(delta == mid, n - 1, 2 * (n - delta) - 1)),
        ).astype(jnp.int32)

    owner = tile_cols // blocks
    spot = jnp.sum(
        jnp.where(owner[..., None] == jnp.arange(n), jnp.asarray(spots, jnp.int32), 0), axis=-1
    )
    rel = slot_of(spot) * blocks + tile_cols % blocks
    inverse = jnp.broadcast_to((1.0 / degrees.astype(F32))[:, None], (nodes, 128))

    unit = 2 * nodes * nodes * half

    def adjacency(first, count):
        return pl.BlockSpec((count * blocks, nodes, tile), lambda i: (first // count, 0, 0))

    whole = lambda shape: pl.BlockSpec(shape, lambda i, *_: (0,) * len(shape))
    wblock = lambda which: pl.BlockSpec((half, half), lambda i, c: ((c[0] + which) % 2, 0))
    rows_spec = whole((nodes, half))
    out_rows = sds((nodes, half), F32)

    place = slot_of(jnp.arange(n, dtype=jnp.int32))
    half_spec = whole((h, half))

    def sum_step(s, came, total):
        return call(
            functools.partial(sum_step_body, blocks),
            out_rows,
            (a, *came, total),
            flops=4 * unit,
            grid=(1,),
            in_specs=[
                pl.BlockSpec(
                    (pl.Element(2 * blocks), pl.Element(nodes), pl.Element(tile)),
                    lambda i: ((2 * s - 1) * blocks, 0, 0),
                )
            ]
            + [half_spec] * 4
            + [rows_spec],
            out_specs=rows_spec,
            name="sum_step",
        )

    part = sds((h, half), F32)
    p = (send_right(features), send_left(features))
    came = [None]
    for s in range(1, mid):
        if s == 1:
            other_rows = lambda w: lax.dynamic_slice(w, ((1 - core) * half, 0), (half, half))
            x_other = swap(features)
            ws_other, wn_other = swap(other_rows(w_self)), swap(other_rows(w_neigh))
            p, rel, inverse, place, x_other, ws_other, wn_other = tie(
                (p, rel, inverse, place, x_other, ws_other, wn_other)
            )
            p = call(
                cut_body,
                (part,) * 4,
                p,
                flops=0,
                grid=(1,),
                in_specs=[rows_spec] * 2,
                out_specs=(half_spec,) * 4,
                name="cut",
            )
            p, q = (p[0], p[3]), (p[1], p[2])
        elif s == 2:
            rel, came[1] = tie((rel, came[1]))
            a, at = call(
                densify_body,
                (sds((n * blocks, nodes, tile), BF16), sds((n * blocks, tile, nodes), BF16)),
                (rel, tile_edges),
                flops=0,
                prefetch=1,
                grid=(blocks,),
                in_specs=[pl.BlockSpec((1, width, tile, tile), lambda b, _: (b, 0, 0, 0))],
                out_specs=(
                    pl.BlockSpec((n * blocks, tile, tile), lambda b, _: (0, b, 0)),
                    pl.BlockSpec((n * blocks, tile, tile), lambda b, _: (0, 0, b)),
                ),
                name="densify",
                vmem=32,
            )
            p, a, at = tie((p, a, at))
        else:
            total = sum_step(s - 2, came[s - 2], total)
            p, total = tie((p, total))
        first = p
        p = (send_right(p[0]), send_left(p[1]))
        if s == 2:
            features_, first = tie((features, first))
            base = call(
                self_body,
                out_rows,
                (ci, features_, x_other, w_self, w_self, bias[None]),
                flops=3 * unit,
                prefetch=1,
                grid=(1,),
                in_specs=[rows_spec, rows_spec, wblock(0), wblock(1), whole((1, half))],
                out_specs=rows_spec,
                name="self_product",
            )
            total = call(
                functools.partial(sum_own_body, blocks),
                out_rows,
                (a, features_),
                flops=2 * unit,
                grid=(1,),
                in_specs=[adjacency(0, 1), rows_spec],
                out_specs=rows_spec,
                name="sum_own",
            )

            q, base, total, ws_other, wn_other = tie((q, base, total, ws_other, wn_other))
        came.append((first[0], q[0], q[1], first[1]))
        if s < mid - 1:
            q = (send_right(q[0]), send_left(q[1]))
    for s in range(mid - 2, mid):
        total = sum_step(s, came[s], total)
    xa, xb = p

    mean = call(
        functools.partial(mean_body, blocks),
        out_rows,
        (a, xa, xb, total, inverse),
        flops=2 * unit,
        grid=(1,),
        in_specs=[adjacency(n - 1, 1), whole((h, half)), whole((h, half)), rows_spec, whole((nodes, 128))],
        out_specs=rows_spec,
        name="mean",
    )
    mean_other = swap(mean)
    base = call(
        own_product_body,
        out_rows,
        (ci, mean, w_neigh, base),
        flops=1.5 * unit,
        prefetch=1,
        grid=(1,),
        in_specs=[rows_spec, wblock(0), rows_spec],
        out_specs=rows_spec,
        name="mean_product",
    )
    hidden, grad_pre = call(
        activate_body,
        (out_rows, out_rows),
        (ci, mean_other, w_neigh, base, cotangent),
        flops=1.5 * unit,
        prefetch=1,
        grid=(1,),
        in_specs=[rows_spec, wblock(1), rows_spec, rows_spec],
        out_specs=(rows_spec, rows_spec),
        name="activate",
    )
    g_other = swap(grad_pre)
    per = 2 * half // n
    shard = 2 * per + 8
    grads, first = call(
        functools.partial(weight_body, n),
        (sds((n, shard, half), F32), sds((shard, half), F32)),
        (place, features, x_other, mean, mean_other, grad_pre),
        flops=6 * unit,
        prefetch=1,
        grid=(1,),
        in_specs=[rows_spec] * 5,
        out_specs=(whole((n, shard, half)), whole((shard, half))),
        name="weight_grads",
    )
    g_other, first = tie((g_other, first))
    direct_own, mean_own = call(
        own_back_body,
        (out_rows, out_rows),
        (ci, grad_pre, w_self, w_neigh),
        flops=3 * unit,
        prefetch=1,
        grid=(1,),
        in_specs=[rows_spec, wblock(0), wblock(0)],
        out_specs=(rows_spec, rows_spec),
        name="back_own",
    )
    part = sds((h, half), F32)
    high, low, *out = call(
        functools.partial(scaled_body, blocks),
        (sds((nodes, half), BF16), sds((nodes, half), BF16)) + (part,) * 4,
        (g_other, wn_other, mean_own, inverse, at),
        flops=3.5 * unit,
        grid=(1,),
        in_specs=[
            rows_spec,
            whole((half, half)),
            rows_spec,
            whole((nodes, 128)),
            pl.BlockSpec(
                (pl.Element(3 * blocks), pl.Element(tile), pl.Element(nodes)),
                lambda i: ((n - 3) * blocks, 0, 0),
            ),
        ],
        out_specs=(rows_spec, rows_spec) + (half_spec,) * 4,
        name="scaled",
    )
    ta, tb, *second = out
    w = (send_right(first),)
    terms = call(
        terms_body,
        sds((n - 1, nodes, half), F32),
        (at, high, low),
        flops=2 * unit * (n - 1),
        grid=(n - 1,),
        in_specs=[pl.BlockSpec((blocks, tile, nodes), lambda i: (n - 2 - i, 0, 0)), rows_spec, rows_spec],
        out_specs=pl.BlockSpec((1, nodes, half), lambda i: (n - 2 - i, 0, 0)),
        name="terms",
    )
    result = call(
        direct_body,
        out_rows,
        (g_other, ws_other, direct_own, terms),
        flops=1.5 * unit,
        grid=(1,),
        in_specs=[rows_spec, whole((half, half)), rows_spec, pl.BlockSpec((1, nodes, half), lambda i: (0, 0, 0))],
        out_specs=rows_spec,
        name="direct",
    )

    def join(source, right_at, left_at, rows, came, name):
        out = sds((rows, half), F32)
        block = lambda at: pl.BlockSpec((1, rows, half), lambda i: (*at, 0))
        return call(
            join_body,
            (out, out),
            (source, source, *came),
            flops=0,
            grid=(1,),
            in_specs=[block(right_at), block(left_at)] + [whole((rows, half))] * len(came),
            out_specs=(whole(out.shape), whole(out.shape)),
            name=name,
        )

    def weight_step(step, w):
        if step < mid:
            d = mid - step
            return join(grads, (2 * d, 0), (2 * d - 1, 0), shard, w, "join_weights")
        if step > mid:
            return w
        mine, bias_sum = call(
            mine_body,
            (sds((2 * per, half), F32), sds((1, half), F32)),
            (grads, *w),
            flops=0,
            grid=(1,),
            in_specs=[pl.BlockSpec((1, shard, half), lambda i: (0, 0, 0))] + [whole((shard, half))] * 2,
            out_specs=(whole((2 * per, half)), whole((1, half))),
            name="mine",
        )
        shards.append(mine)
        biases.append(bias_sum)
        return mine, mine

    shards, biases = [], []
    chains = [(), second]
    for step in range(1, 2 * mid):
        w_in = weight_step(step, w)
        f_in = None
        turn = step - 1
        which = turn % 2
        d = mid - (turn + 1) // 2
        if turn == 0:
            f_in = ta, tb
        elif turn == 1:
            f_in = tuple(second)
        elif turn < 2 * mid - 1:
            at = ((2 * d, which), (2 * d - 1, 1 - which))
            f_in = join(terms, *at, h, chains[which], "join_terms")
        if step == 2:
            result, w_in = tie((result, w_in))
        if f_in is not None and step > 1:
            w_in, f_in = tie((w_in, f_in))
        w = (send_right(w_in[0]), send_left(w_in[1])) if step < 2 * mid - 1 else (send_right(w_in[0]),)
        if step >= mid:
            shards += w
        if f_in is not None:
            chains[which] = (send_right(f_in[0]), send_left(f_in[1]))
    p, q = chains
    grad_bias = biases[0]

    steps = [0]
    for s in range(1, mid):
        steps += [-s, s]
    steps.append(mid)
    where = ((me + jnp.asarray(steps, jnp.int32)) % n + core * mid) % n
    where = where.astype(jnp.int32)
    grad_features = call(
        final_body,
        out_rows,
        (result, p[0], q[1], q[0], p[1]),
        flops=0,
        grid=(1,),
        in_specs=[rows_spec] + [half_spec] * 4,
        out_specs=rows_spec,
        name="final",
    )
    out_shard = sds((n, per, half), F32)
    *early, late = shards
    grad_self, grad_neigh = call(
        assemble_body,
        (out_shard, out_shard),
        (where, *early),
        flops=0,
        prefetch=1,
        grid=(1,),
        in_specs=[whole((2 * per, half))] * (n - 1),
        out_specs=(whole((n, per, half)), whole((n, per, half))),
        name="assemble",
    )
    late, grad_self, grad_neigh, grad_features = tie((late, grad_self, grad_neigh, grad_features))
    last_spec = pl.BlockSpec((1, per, half), lambda i, where: (where[n - 1], 0, 0))
    grad_self, grad_neigh = call(
        place_body,
        (out_shard, out_shard),
        (where, late, grad_self, grad_neigh),
        flops=0,
        prefetch=1,
        grid=(1,),
        in_specs=[whole((2 * per, half))] + [pl.BlockSpec(memory_space=pl.ANY)] * 2,
        out_specs=(last_spec, last_spec),
        name="place_last",
        aliases={2: 0, 3: 1},
    )
    return (
        hidden,
        grad_features,
        grad_self.reshape(2 * half, half),
        grad_neigh.reshape(2 * half, half),
        grad_bias.reshape(half),
    )


def solution(mesh):
    n = mesh.shape["rows"]
    coords = [d.coords for d in mesh.devices[0, :, 0]]
    axes = sum(len(set(c)) > 1 for c in zip(*coords))
    if axes > 1:
        order = list(range(0, n, 2)) + list(range(n - 1, 0, -2))
    else:
        order = list(range(n))
    return jax.shard_map(
        functools.partial(local, order),
        mesh=mesh,
        in_specs=(
            P(("groups", "rows"), "cols"),
            P(("groups", "rows"), None),
            P(("groups", "rows"), None, None, None),
            P(("groups", "rows")),
            P(None, "cols"),
            P(None, "cols"),
            P("cols"),
            P(("groups", "rows"), "cols"),
        ),
        out_specs=(
            P(("groups", "rows"), "cols"),
            P(("groups", "rows"), "cols"),
            P("groups", "cols"),
            P("groups", "cols"),
            P(("groups", "cols")),
        ),
        check_vma=False,
    )
```
